512 devices in a mesh: idx: 64 (over y, z), cur: 4 (over x), spin: 2 (over core).
Axes of the slice: x: 4, y: 8, z: 8, core: 2. Of those that a mesh axis runs over, the one named last changes fastest.
Arguments:
- elemental: bfloat16 [1, 2, 192, 192, 192], P(None, None, 'idx'), may hold values from -6 to 6
- peramb_one: bfloat16 [4, 2, 192, 192], P('spin', None, 'idx'), may hold values from -0.3125 to 0.3125
- peramb_two: bfloat16 [4, 2, 192, 192], P('spin', None, 'idx'), may hold values from -0.3125 to 0.3125
- gen_peramb: bfloat16 [4, 4, 2, 192, 192], P('cur', 'spin', None, 'idx'), may hold values from -0.3125 to 0.3125
Outputs:
- sink_tensor: float32 [1, 4, 4, 2, 192, 192, 192], P(None, 'cur', 'spin', None, 'idx')
The draws below stay inside these ranges and needn't reach their ends.
All inputs are finite; a program needn't handle non-finite values.
Results may differ from the reference program's by a relative error of at most 0.00065.
Values may be sent and summed in bfloat16 or wider, within the bound.
A program may use at most 64 MiB of HBM per device.

```python
import jax
import jax.numpy as jnp
from jax import lax

N = 192
MOM = 1
CURRENTS = 4
SPIN = 4


def block_levels(rng, extent, shards, low, largest):
    gain, own = 1.0, jax.random.fold_in(rng, 6)
    for dim, blocks in shards:
        draws = jnp.exp(jax.random.uniform(jax.random.fold_in(own, dim), (blocks,), jnp.float32, low / len(shards), largest / len(shards)))
        gain = gain * jnp.repeat(draws, extent[dim] // blocks).reshape([-1 if axis == dim else 1 for axis in range(len(extent))])
    return gain


def centred(own_key, shape, width, most, pieces=(), dtype=jnp.bfloat16):
    entries = width * jax.random.normal(own_key, shape, jnp.float32)
    if pieces:
        entries = entries * block_levels(own_key, shape, pieces, -0.22, 0.18)
    return jnp.clip(entries, -most, most).astype(dtype)


def setup_inputs(seed: int = 0) -> dict:
    seeds = jax.random.split(jax.random.key(seed), 5)
    return {
        "elemental": centred(seeds[0], (MOM, 2, N, N, N), 1.0, 6.0, ((2, 64),)),
        "peramb_one": centred(seeds[1], (SPIN, 2, N, N), (2 * N) ** -0.5, 0.3125, ((0, 2), (2, 64))),
        "peramb_two": centred(seeds[2], (SPIN, 2, N, N), (2 * N) ** -0.5, 0.3125, ((0, 2), (2, 64))),
        "gen_peramb": centred(seeds[3], (CURRENTS, SPIN, 2, N, N), (2 * N) ** -0.5, 0.3125, ((0, 4), (1, 2), (3, 64))),
    }


def blocks(values):
    real_part = values[..., 0, :, :]
    imag_part = values[..., 1, :, :]
    upper_half = jnp.stack([real_part, imag_part], axis=-2)
    lower_half = jnp.stack([-imag_part, real_part], axis=-2)
    return jnp.stack([upper_half, lower_half], axis=-4)


def reference(elemental, peramb_one, peramb_two, gen_peramb):
    highest = lax.Precision.HIGHEST
    one_block = blocks(peramb_one.astype(jnp.float32))
    two_block = blocks(peramb_two.astype(jnp.float32))
    gen_block = blocks(gen_peramb.astype(jnp.float32))
    by_moment = []
    for moment in range(MOM):
        source = elemental[moment].astype(jnp.float32)
        by_current = []
        for current in range(CURRENTS):
            by_spin = []
            for spin_comp in range(SPIN):
                tensor = jnp.einsum("rabc,rcRd->Rabd", source, gen_block[current, spin_comp], precision=highest)
                tensor = jnp.einsum("rabd,rbRe->Raed", tensor, two_block[spin_comp], precision=highest)
                tensor = jnp.einsum("raed,raRf->Rfed", tensor, one_block[spin_comp], precision=highest)
                by_spin.append(tensor)
            by_current.append(jnp.stack(by_spin, axis=0))
        by_moment.append(jnp.stack(by_current, axis=0))
    return jnp.stack(by_moment, axis=0)
```

```python
import jax
import jax.numpy as jnp
from jax import lax
from jax.experimental import pallas as pl
from jax.experimental.pallas import tpu as pltpu
from jax.sharding import PartitionSpec as P

MESH = pl.DeviceIdType.MESH
F32, BF16 = jnp.float32, jnp.bfloat16
TN = (((0,), (0,)), ((), ()))
POWER = 32768.0


def kernel(
    e_ref, p_ref, qg_ref, out_ref,
    ef, e1, p1, qg0, qg1, ebuf, psend, pbuf, qgbuf, xs, xb, xf, ah, al, zr, zi, qt, gw,
    own_sem, e1s, e1r, p1s, p1r, q1s, q1r, e2s, e2r, p2s, p2r, q2s, q2r, x4s, x4r, x5s, x5r,
):
    idx, x, k = lax.axis_index("idx"), lax.axis_index("cur"), lax.axis_index("spin")
    y, z = idx // 8, idx % 8
    u = y * (1 - k) + z * k
    v = z * (1 - k) + y * k

    def column(uu, vv):
        return (uu * (1 - k) + vv * k) * 8 + vv * (1 - k) + uu * k

    def on_u(d):
        return (u + d) % 8

    def on_v(d):
        return (v + d) % 8

    def send(src, dst, ss, rs, where):
        return pltpu.make_async_remote_copy(
            src_ref=src, dst_ref=dst, send_sem=ss, recv_sem=rs, device_id=where, device_id_type=MESH
        )

    barrier = pltpu.get_barrier_semaphore()
    for d in range(1, 8):
        pl.semaphore_signal(barrier, inc=1, device_id=(column(on_u(d), v), x, k), device_id_type=MESH)
    for d in range(1, 8):
        pl.semaphore_signal(barrier, inc=1, device_id=(column(u, on_v(d)), x, k), device_id_type=MESH)
    for d in range(1, 4):
        pl.semaphore_signal(barrier, inc=1, device_id=(idx, (x + d) % 4, k), device_id_type=MESH)

    ef[0] = e_ref[:, :, :128].astype(F32)
    ef[1, :, :, :64] = e_ref[:, :, 128:].astype(F32)
    for n in range(3):
        qg0[n] = qg_ref[:, 128 * n:128 * n + 128].astype(F32)
    pl.semaphore_wait(barrier, 17)

    def rows_of(uu, h):
        return 24 * (uu * (1 - k) + (2 * x + h) * k) + 3 * ((2 * x + h) * (1 - k) + uu * k)

    sends = []
    for d in range(1, 8):
        to = on_u(d)
        for h in range(2):
            sends.append(send(
                ef.at[:, :, pl.ds(rows_of(to, h), 3), :], e1.at[:, :, pl.ds(3 * h, 3), u, :],
                e1s.at[d - 1, h], e1r.at[d - 1, h], (column(to, v), x, k)))
            sends[-1].start()
    psends, qsends = [], []
    for d in range(1, 8):
        psends.append(send(p_ref, p1.at[:, :, u, :], p1s.at[d - 1], p1r.at[d - 1], (column(on_u(d), v), x, k)))
        psends[-1].start()
    for d in range(1, 8):
        qsends.append(send(qg0, qg1.at[:, :, u, :], q1s.at[d - 1], q1r.at[d - 1], (column(on_u(d), v), x, k)))
        qsends[-1].start()
    own = [
        pltpu.make_async_copy(ef.at[:, :, pl.ds(rows_of(u, h), 3), :], e1.at[:, :, pl.ds(3 * h, 3), u, :], own_sem.at[h])
        for h in range(2)
    ]
    own.append(pltpu.make_async_copy(p_ref, p1.at[:, :, u, :], own_sem.at[2]))
    own.append(pltpu.make_async_copy(qg0, qg1.at[:, :, u, :], own_sem.at[3]))
    for c in own:
        c.start()

    for c in own[:2] + sends:
        c.wait()
    for j in range(3):
        last = jnp.concatenate([e1[1, :, 2 * j, :, :64], e1[1, :, 2 * j + 1, :, :64]], axis=2)
        for n, tile in enumerate((e1[0, :, 2 * j], e1[0, :, 2 * j + 1], last)):
            ebuf[v, :, pl.ds(384 * j + 128 * n, 128)] = tile.reshape(48, 128).astype(BF16)
    sends2 = []
    for d in range(1, 8):
        sends2.append(send(ebuf.at[v], ebuf.at[v], e2s.at[d - 1], e2r.at[d - 1], (column(u, on_v(d)), x, k)))
        sends2[-1].start()
    for c in [own[2]] + psends:
        c.wait()
    for n in range(8):
        psend[n] = p1[:, n].reshape(48, 128).astype(BF16)
    for d in range(1, 8):
        sends2.append(send(psend.at[on_v(d)], pbuf.at[v], p2s.at[d - 1], p2r.at[d - 1], (column(u, on_v(d)), x, k)))
        sends2[-1].start()
    pbuf[v] = psend[v]
    for c in [own[3]] + qsends:
        c.wait()
    for n in range(3):
        qgbuf[v, :, pl.ds(128 * n, 128)] = qg1[n].reshape(96, 128).astype(BF16)
    for c in sends2:
        c.wait()

    value = lax.dot_general(
        pbuf[...].reshape(384, 128), ebuf[...].reshape(384, 1152), TN, preferred_element_type=F32)
    largest = jnp.maximum(jnp.max(jnp.abs(value)), 1e-30)
    largest = jnp.full((128, 1152), largest, F32).astype(BF16).astype(F32)
    scaled = value * (POWER / largest)
    square = scaled * scaled
    fourth = square * square
    coded = jnp.where(scaled < 0, -fourth, fourth) * fourth
    row = lax.broadcasted_iota(jnp.int32, (128, 1152), 0) % 16
    xs[...] = jnp.where(row == 12, largest, coded).astype(BF16).reshape(8, 16, 1152)

    sends4 = []
    for d in range(1, 8):
        sends4.append(send(xs.at[on_u(d)], xb.at[x, u], x4s.at[d - 1], x4r.at[d - 1], (column(on_u(d), v), x, k)))
        sends4[-1].start()
    sendsq = []
    for d in range(1, 8):
        sendsq.append(send(qgbuf.at[v], qgbuf.at[v], q2s.at[d - 1], q2r.at[d - 1], (column(u, on_v(d)), x, k)))
        sendsq[-1].start()
    xb[x, u] = xs[u]
    sends5 = []

    def forward(d):
        block = (u - d + 8) % 8
        for s in range(1, 4):
            sends5.append(send(
                xb.at[x, block], xb.at[x, block], x5s.at[s - 1, d], x5r.at[s - 1, d], (idx, (x + s) % 4, k)))
            sends5[-1].start()

    forward(0)
    for d in range(1, 8):
        sends4[d - 1].wait()
        forward(d)
    for c in sendsq:
        c.wait()

    received = lax.broadcasted_iota(jnp.int32, (192, 192), 0)
    wanted = lax.broadcasted_iota(jnp.int32, (192, 192), 1)
    rv, rt, ru = received // 24, received // 8 % 3, received % 8
    natural = rt + 3 * (rv * (1 - k) + ru * k) + 24 * (ru * (1 - k) + rv * k)
    place_g = jnp.where(natural == wanted, 1.0, 0.0).astype(BF16)
    beta = 3 * (rv % 2) + rt
    order = (beta % 2) * 96 + (beta // 2) * 32 + (rv // 2) * 8 + ru
    place_q = jnp.where(order == wanted, 1.0, 0.0).astype(BF16)
    none = jnp.zeros((64, 192), BF16)
    for s in range(2):
        qs, gs = [], []
        for r in range(2):
            part = jnp.concatenate(
                [qgbuf[n, pl.ds(48 * s + 24 * r, 24), :].astype(F32) for n in range(8)], axis=0).astype(BF16)
            qs.append(lax.dot_general(part[:, :192], place_q, TN, preferred_element_type=F32).astype(BF16))
            gs.append(lax.dot_general(place_g, part[:, 192:], TN, preferred_element_type=F32).astype(BF16))
        qr, qi = qs
        qt[s, 0, :, :192], qt[s, 0, :, 192:] = qr, -qi
        qt[s, 1, :, :192], qt[s, 1, :, 192:] = qi, qr
        for odd in range(2):
            gr, gi = [
                jnp.concatenate([g[:128], none, g[128:]] if odd else [g, none], axis=0) for g in gs
            ]
            gw[s, odd, 0, :256], gw[s, odd, 0, 256:] = gr, -gi
            gw[s, odd, 1, :256], gw[s, odd, 1, 256:] = gi, gr

    for c in sends5:
        c.wait()
    for n in range(9):
        xf[n] = xb[:, :, :, 128 * n:128 * n + 128].astype(F32).reshape(512, 128)

    scale = xf[0, pl.ds(12, 32, stride=16), :] * (1.0 / POWER)
    for s in range(2):
        for t in range(3):
            for r in range(2):
                for n in range(9):
                    j, tile = n // 3, n % 3
                    code = xf[n, pl.ds(4 * t + 2 * s + r, 32, stride=16), :]
                    root = lax.rsqrt(jnp.maximum(jnp.abs(code), 1.2e-38))
                    fourth = lax.rsqrt(root)
                    size = fourth * lax.rsqrt(fourth) * scale
                    value = jnp.where(code < 0, -size, size)
                    high = value.astype(BF16)
                    low = (value - high.astype(F32)).astype(BF16)
                    at = pl.ds(96 * t + 32 * j, 32)
                    for odd in range(2):
                        if tile in (odd, 2):
                            lane = pl.ds(256 * r + (128 if tile == 2 else 0), 128)
                            ah[odd, at, lane] = high
                            al[odd, at, lane] = low
        for odd in range(2):
            for part, dst in ((0, zr), (1, zi)):
                w = gw[s, odd, part]
                dst[odd] = jnp.dot(ah[odd], w, preferred_element_type=F32) + jnp.dot(
                    al[odd], w, preferred_element_type=F32)
        for t in range(3):
            at = pl.ds(96 * t, 96)
            zc = jnp.concatenate([zr[0, at], zr[1, at], zi[0, at], zi[1, at]], axis=0)
            high = zc.astype(BF16)
            low = (zc - high.astype(F32)).astype(BF16)
            for r in range(2):
                q = qt[s, r]
                out_ref[s, r, t] = jnp.dot(q, high, preferred_element_type=F32) + jnp.dot(
                    q, low, preferred_element_type=F32)


def body(elemental, peramb_one, peramb_two, gen_peramb):
    core = lax.axis_index("spin")
    e = elemental.reshape(6, 192, 192)
    p = peramb_one.astype(F32).reshape(2, 2, 3, 8, 8, 3)
    p = jnp.where(core == 0, p, jnp.swapaxes(p, 3, 4))
    p = jnp.stack([p, jnp.stack([-p[:, 1], p[:, 0]], axis=1)], axis=0)
    p = jnp.transpose(p, (0, 3, 5, 4, 6, 1, 2)).reshape(6, 8, 8, 12)
    p = jnp.pad(p, ((0, 0), (0, 0), (0, 0), (0, 4))).reshape(6, 8, 128)
    qg = jnp.concatenate([peramb_two.reshape(12, 192), gen_peramb.reshape(12, 192)], axis=1)
    dma = pltpu.SemaphoreType.DMA
    vmem = pl.BlockSpec(memory_space=pltpu.VMEM)
    out = pl.pallas_call(
        kernel,
        out_shape=jax.ShapeDtypeStruct((2, 2, 3, 192, 192), F32),
        in_specs=[vmem] * 3,
        out_specs=vmem,
        scratch_shapes=[
            pltpu.VMEM((2, 6, 192, 128), F32),
            pltpu.VMEM((2, 6, 6, 8, 128), F32),
            pltpu.VMEM((6, 8, 8, 128), F32),
            pltpu.VMEM((3, 12, 128), F32),
            pltpu.VMEM((3, 12, 8, 128), F32),
            pltpu.VMEM((8, 48, 1152), BF16),
            pltpu.VMEM((8, 48, 128), BF16),
            pltpu.VMEM((8, 48, 128), BF16),
            pltpu.VMEM((8, 96, 384), BF16),
            pltpu.VMEM((8, 16, 1152), BF16),
            pltpu.VMEM((4, 8, 16, 1152), BF16),
            pltpu.VMEM((9, 512, 128), F32),
            pltpu.VMEM((2, 288, 512), BF16),
            pltpu.VMEM((2, 288, 512), BF16),
            pltpu.VMEM((2, 288, 192), F32),
            pltpu.VMEM((2, 288, 192), F32),
            pltpu.VMEM((2, 2, 192, 384), BF16),
            pltpu.VMEM((2, 2, 2, 512, 192), BF16),
            dma((4,)),
            dma((7, 2)), dma((7, 2)), dma((7,)), dma((7,)), dma((7,)), dma((7,)),
            dma((7,)), dma((7,)), dma((7,)), dma((7,)), dma((7,)), dma((7,)),
            dma((7,)), dma((7,)), dma((3, 8)), dma((3, 8)),
        ],
        compiler_params=pltpu.CompilerParams(
            collective_id=0, has_side_effects=True, vmem_limit_bytes=48 << 20),
        name="sink",
    )(e, p, qg)
    return out.reshape(1, 1, 2, 2, 3, 192, 192)


def solution(mesh):
    return jax.shard_map(
        body,
        mesh=mesh,
        in_specs=(
            P(None, None, "idx", None, None),
            P("spin", None, "idx", None),
            P("spin", None, "idx", None),
            P("cur", "spin", None, "idx", None),
        ),
        out_specs=P(None, "cur", "spin", None, "idx", None, None),
        check_vma=False,
    )
```

```python
import jax
import jax.numpy as jnp
from jax import lax
from jax.experimental import pallas as pl
from jax.experimental.pallas import tpu as pltpu
from jax.sharding import PartitionSpec as P

MESH = pl.DeviceIdType.MESH
F32, BF16 = jnp.float32, jnp.bfloat16
TN = (((0,), (0,)), ((), ()))
POWER = 32768.0
RELAY_V = True
RELAY_X = False
FAR_FIRST = (4, 3, 5, 2, 6, 1, 7)
SLOT = {1: 2, 2: 3, 3: 1}


def kernel(
    e_hbm, p_hbm, q_hbm, g_hbm, out_ref,
    e_ref, p_ref, q_ref, g_ref, e0, e1, ef, p0, p1, pf, qg0, qg1, qf,
    eba, ebb, psend, pbuf, qgbuf, xsa, xsb, xba, xbb, xf, xr, ah, zr, zi, qt, gw,
    in_sem, e1s, e1r, p1s, p1r, q1s, q1r, eas, ear, ebs, ebr, p2s, p2r, q2s, q2r,
    xas, xar, xbs, xbr, fas, far, fbs, fbr,
):
    idx, x, k = lax.axis_index("idx"), lax.axis_index("cur"), lax.axis_index("spin")
    y, z = idx // 8, idx % 8
    u = y * (1 - k) + z * k
    v = z * (1 - k) + y * k

    def column(uu, vv):
        return (uu * (1 - k) + vv * k) * 8 + vv * (1 - k) + uu * k

    def on_u(d):
        return (u + d) % 8

    def on_v(d):
        return (v + d) % 8

    def send(src, dst, ss, rs, where):
        copy = pltpu.make_async_remote_copy(
            src_ref=src, dst_ref=dst, send_sem=ss, recv_sem=rs, device_id=where, device_id_type=MESH
        )
        copy.start()
        return copy

    def to_u(d):
        return column(on_u(d), v), x, k

    def to_v(d):
        return column(u, on_v(d)), x, k

    loads = [
        pltpu.make_async_copy(src, dst, in_sem.at[i])
        for i, (src, dst) in enumerate(((e_hbm, e_ref), (p_hbm, p_ref), (q_hbm, q_ref), (g_hbm, g_ref)))
    ]
    for c in loads:
        c.start()
    barrier = pltpu.get_barrier_semaphore()
    for d in FAR_FIRST:
        pl.semaphore_signal(barrier, inc=1, device_id=to_u(d), device_id_type=MESH)
        pl.semaphore_signal(barrier, inc=1, device_id=to_v(d), device_id_type=MESH)
    for d in (2, 1, 3):
        pl.semaphore_signal(barrier, inc=1, device_id=(idx, (x + d) % 4, k), device_id_type=MESH)

    row = lax.broadcasted_iota(jnp.int32, (64, 192), 0)
    uu, beta = row // 8, row % 8
    h, t = beta // 3, beta % 3
    source = 24 * (uu * (1 - k) + (2 * x + h) * k) + 3 * ((2 * x + h) * (1 - k) + uu * k) + t
    pick = jnp.where(
        (source == lax.broadcasted_iota(jnp.int32, (64, 192), 1)) & (beta < 6), 1.0, 0.0).astype(BF16)
    loads[0].wait()
    picked = [jnp.dot(pick, e_ref[i], preferred_element_type=F32) for i in range(6)]
    e0[...] = jnp.concatenate(
        [m[:, :128].reshape(8, 8, 128) for m in picked]
        + [
            jnp.concatenate([picked[2 * i][:, 128:], picked[2 * i + 1][:, 128:]], axis=1).reshape(8, 8, 128)
            for i in range(3)
        ]
        + [jnp.zeros((8, 8, 128), F32)], axis=1).astype(BF16)
    f = lax.broadcasted_iota(jnp.int32, (192, 1024), 0)
    n = lax.broadcasted_iota(jnp.int32, (192, 1024), 1)
    nv, nu, nt = n // 128, n // 16 % 8, n // 4 % 4
    owner = 8 * (nu * (1 - k) + nv * k) + nv * (1 - k) + nu * k
    pick = jnp.where((3 * owner + nt == f) & (nt < 3) & (n % 4 == 0), 1.0, 0.0).astype(BF16)
    for c in loads[1:]:
        c.wait()
    p = p_ref[...].astype(F32)
    p = jnp.concatenate([p[s, :, r, :] for s in range(2) for r in range(2)], axis=0)
    spread = jnp.dot(p.astype(BF16), pick, preferred_element_type=F32)
    by = [spread] + [pltpu.roll(spread, i, 1) for i in range(1, 4)]
    upper = by[0][0:3] + by[1][3:6] + by[2][6:9] + by[3][9:12]
    lower = by[1][0:3] - by[0][3:6] + by[3][6:9] - by[2][9:12]
    both = jnp.concatenate([upper, lower, jnp.zeros((2, 1024), F32)], axis=0)
    p0[...] = jnp.concatenate([both[:, 128 * i:128 * i + 128] for i in range(8)], axis=0).astype(BF16)
    qg0[...] = jnp.concatenate([
        jnp.concatenate([a[s, :, r, :] for s in range(2) for r in range(2)] + [jnp.zeros((4, 192), F32)], axis=0)
        for a in (q_ref[...].astype(F32), g_ref[...].astype(F32))
    ], axis=1).astype(BF16)
    pl.semaphore_wait(barrier, 17)

    e_sends = [send(e0.at[on_u(d)], e1.at[u], e1s.at[d - 1], e1r.at[d - 1], to_u(d)) for d in FAR_FIRST]
    p_sends = [send(p0, p1.at[u], p1s.at[d - 1], p1r.at[d - 1], to_u(d)) for d in FAR_FIRST]
    e1[u] = e0[u]
    p1[u] = p0[...]
    qg1[u] = qg0[...]

    left = lax.broadcasted_iota(jnp.int32, (8, 128), 1) < 64

    def tile(m):
        j, m = m // 3, m % 3
        pieces = []
        for i in range(6):
            if m < 2:
                pieces.append(ef[pl.ds(8 * i + 2 * j + m, 8, stride=80), :])
                continue
            first, second = [ef[pl.ds(48 + 8 * (i // 2) + 2 * j + b, 8, stride=80), :] for b in range(2)]
            if i % 2 == 0:
                second = pltpu.roll(second, 64, 1)
            else:
                first = pltpu.roll(first, 64, 1)
            pieces.append(jnp.where(left, first, second))
        return jnp.concatenate(pieces, axis=0).astype(BF16)

    for c in e_sends:
        c.wait()
    ef[...] = e1[...].astype(F32).reshape(640, 128)
    for m in range(4):
        eba[v, :, pl.ds(128 * m, 128)] = tile(m)
    def first_leg(block, ss, rs):
        return {
            d: send(block.at[v], block.at[v], ss.at[d - 1], rs.at[d - 1], to_v(d))
            for d in ((2, 6, 1, 7) if RELAY_V else FAR_FIRST)
        }

    def second_leg(block, cut, sent, ss, rs):
        if not RELAY_V:
            return []
        size = block.shape[2]
        more = []
        for d, near, lanes, place in ((2, 1, pl.ds(0, cut), 3), (6, 7, pl.ds(cut, size - cut), 7)):
            sent[d].wait()
            came = (v - d + 8) % 8
            whole, part = block.at[came], block.at[came, :, lanes]
            more.append(send(whole, whole, ss.at[2 if d == 2 else 4], rs.at[2 if d == 2 else 4], to_v(near)))
            more.append(send(part, part, ss.at[place], rs.at[place], to_v(d)))
        return [sent[1], sent[7]] + more

    a_sent = first_leg(eba, eas, ear)
    for c in p_sends:
        c.wait()
    pf[...] = p1[...].astype(F32).reshape(512, 128)
    for i in range(8):
        psend[i] = jnp.concatenate(
            [pf[pl.ds(8 * i + r, 8, stride=64), :] for r in range(6)], axis=0).astype(BF16)
    a_sends = [send(psend.at[on_v(d)], pbuf.at[v], p2s.at[d - 1], p2r.at[d - 1], to_v(d)) for d in FAR_FIRST]
    pbuf[v] = psend[v]
    for m in range(5):
        ebb[v, :, pl.ds(128 * m, 128)] = tile(4 + m)
    b_sent = first_leg(ebb, ebs, ebr)
    q_sends = [send(qg0, qg1.at[u], q1s.at[d - 1], q1r.at[d - 1], to_u(d)) for d in FAR_FIRST]
    if RELAY_V:
        a_sends += second_leg(eba, 256, a_sent, eas, ear)
        b_sends = second_leg(ebb, 384, b_sent, ebs, ebr)
    else:
        a_sends += list(a_sent.values())
        b_sends = list(b_sent.values())

    weights = None

    def contract(part, tiles):
        value = lax.dot_general(weights, part[...].reshape(384, 128 * tiles), TN, preferred_element_type=F32)
        largest = jnp.maximum(jnp.max(jnp.abs(value)), 1e-30)
        largest = jnp.full((8, 8, 128), largest, F32).astype(BF16).astype(F32)
        halves = []
        for m in range(tiles):
            scaled = value[:, 128 * m:128 * m + 128].reshape(8, 2, 8, 128)
            pair = []
            for i in range(2):
                a = scaled[:, i] * (POWER / largest)
                square = a * a
                fourth = square * square
                pair.append(jnp.where(a < 0, -fourth, fourth) * fourth)
            halves.append(pair)
        return halves, largest

    def along_x(block, there, here, part, sem, ss, rs, s):
        return send(block.at[here, part], block.at[there, part], ss.at[sem], rs.at[sem], (idx, (x + s) % 4, k))

    def spread_x(block, ss, rs):
        return {
            s: along_x(block, SLOT[s], 0, pl.ds(0, 8), s - 1, ss, rs, s) for s in ((1, 3) if RELAY_X else (2, 1, 3))
        }

    def pass_x(block, sent, ss, rs):
        for s in (1, 3):
            sent[s].wait()
        if not RELAY_X:
            return [sent[2]]
        return [
            along_x(block, 3, 2, pl.ds(0, 4), 1, ss, rs, 1), along_x(block, 3, 1, pl.ds(4, 4), 3, ss, rs, 3)
        ]

    def decode(i):
        for m in range(7):
            code = (xba[i, :, :, 128 * m:128 * m + 128] if m < 3 else xbb[i, :, :, 128 * m - 384:128 * m - 256])
            code = code.astype(F32).reshape(128, 128)
            if m == 6:
                xr[pl.ds(128 * i, 128)] = code
            root = lax.rsqrt(jnp.maximum(jnp.abs(code), 1.2e-38))
            fourth = lax.rsqrt(root)
            size = fourth * lax.rsqrt(fourth)
            xf[m, pl.ds(128 * i, 128)] = jnp.where(code < 0, -size, size)

    low_rows = lax.broadcasted_iota(jnp.int32, (8, 8, 128), 1) < 4

    def third(pair, t):
        return pair[0] if t == 1 else pltpu.roll(pair[t // 2], 4, 1)

    def put(dst, m, first, second):
        dst[:, :, 128 * m:128 * m + 128] = jnp.concatenate([first, second], axis=1).astype(BF16)

    for c in a_sends:
        c.wait()
    weights = pbuf[...].reshape(384, 128)
    halves, scale_a = contract(eba, 4)
    for m in range(3):
        put(xsa, m, halves[m][0], jnp.where(low_rows, halves[m][1], third(halves[3], m)))
    xa_sends = [
        send(xsa.at[on_u(d)], xba.at[0, u], xas.at[d - 1], xar.at[d - 1], to_u(d)) for d in FAR_FIRST
    ]
    xba[0, u] = xsa[u]
    for c in b_sends:
        c.wait()
    halves, scale_b = contract(ebb, 5)
    for m in range(3):
        put(xsb, m, halves[m][0], jnp.where(low_rows, halves[m][1], third(halves[4], m)))
    sub = lax.broadcasted_iota(jnp.int32, (8, 8, 128), 1)
    put(xsb, 3, halves[3][0], jnp.where(low_rows, halves[3][1], jnp.where(sub == 4, scale_a, scale_b)))
    xb_sends = [
        send(xsb.at[on_u(d)], xbb.at[0, u], xbs.at[d - 1], xbr.at[d - 1], to_u(d)) for d in FAR_FIRST
    ]
    xbb[0, u] = xsb[u]

    for c in xa_sends:
        c.wait()
    fa_sends = spread_x(xba, fas, far)
    for c in q_sends:
        c.wait()
    for i in range(3):
        qf[i] = qg1[:, :, 128 * i:128 * i + 128].astype(F32).reshape(128, 128)
        qgbuf[v, :, pl.ds(128 * i, 128)] = jnp.concatenate(
            [qf[i, pl.ds(r, 8, stride=16), :] for r in range(12)], axis=0).astype(BF16)
    qg_sends = [send(qgbuf.at[v], qgbuf.at[v], q2s.at[d - 1], q2r.at[d - 1], to_v(d)) for d in FAR_FIRST]
    for c in xb_sends:
        c.wait()
    fb_sends = spread_x(xbb, fbs, fbr)
    fa_more = pass_x(xba, fa_sends, fas, far)
    decode(0)
    fb_more = pass_x(xbb, fb_sends, fbs, fbr)
    for i in (1, 2):
        decode(i)
    received = lax.broadcasted_iota(jnp.int32, (192, 192), 0)
    wanted = lax.broadcasted_iota(jnp.int32, (192, 192), 1)
    rv, rt, ru = received // 24, received // 8 % 3, received % 8
    natural = rt + 3 * (rv * (1 - k) + ru * k) + 24 * (ru * (1 - k) + rv * k)
    place_g = jnp.where(natural == wanted, 1.0, 0.0).astype(BF16)
    beta = 3 * (rv % 2) + rt
    ahead = (rv // 2 - x + 4) % 4
    slot = jnp.where(ahead < 2, ahead, 5 - ahead)
    order = (beta % 2) * 96 + (slot // 2) * 48 + (beta // 2) * 16 + (slot % 2) * 8 + ru
    place_q = jnp.where(order == wanted, 1.0, 0.0).astype(BF16)
    none = jnp.zeros((64, 192), BF16)
    for c in qg_sends:
        c.wait()
    for s in range(2):
        qs, gs = [], []
        for r in range(2):
            part = jnp.concatenate(
                [qgbuf[i, pl.ds(48 * s + 24 * r, 24), :].astype(F32) for i in range(8)], axis=0).astype(BF16)
            qs.append(lax.dot_general(part[:, :192], place_q, TN, preferred_element_type=F32).astype(BF16))
            gs.append(lax.dot_general(place_g, part[:, 192:], TN, preferred_element_type=F32).astype(BF16))
        qr, qi = qs
        qt[s, :192, :192], qt[s, :192, 192:] = qr, -qi
        qt[s, 192:, :192], qt[s, 192:, 192:] = qi, qr
        for odd in range(2):
            gr, gi = [
                jnp.concatenate([m[:128], none, m[128:]] if odd else [m, none], axis=0) for m in gs
            ]
            gw[s, odd, 0, :256], gw[s, odd, 0, 256:] = gr, -gi
            gw[s, odd, 1, :256], gw[s, odd, 1, 256:] = gi, gr

    for half in range(2):
        if half == 1:
            for c in fa_more + fb_more:
                c.wait()
            decode(3)
        scales = [xr[pl.ds(256 * half + 12 + i, 16, stride=16), :] * (1.0 / POWER) for i in range(2)]
        for s in range(2):
            for t in range(3):
                for r in range(2):
                    for m in range(9):
                        if m in (3, 8):
                            place, row = t if m == 3 else 3 + t, 12 + 2 * s + r
                        else:
                            place, row = m if m < 3 else m - 1, 4 * t + 2 * s + r
                        j, kind = m // 3, m % 3
                        code = xf[place, pl.ds(256 * half + row, 16, stride=16), :]
                        value = code * scales[0 if m < 4 else 1]
                        high = value.astype(BF16)
                        low = (value - high.astype(F32)).astype(BF16)
                        at = pl.ds(48 * t + 16 * j, 16)
                        for odd in range(2):
                            if kind in (odd, 2):
                                lane = pl.ds(256 * r + (128 if kind == 2 else 0), 128)
                                ah[s, odd, at, lane] = high
                                ah[s, odd, pl.ds(144 + 48 * t + 16 * j, 16), lane] = low
        for s in range(2):
            for odd in range(2):
                for part, dst in ((0, zr), (1, zi)):
                    w = gw[s, odd, part]
                    both = jnp.dot(ah[s, odd], w, preferred_element_type=F32)
                    dst[s, odd, pl.ds(144 * half, 144)] = both[:144] + both[144:]

    for s in range(2):
        for t in range(3):
            zc = jnp.concatenate([
                m[s, odd, pl.ds(144 * half + 48 * t, 48)] for m in (zr, zi) for odd in range(2) for half in range(2)
            ], axis=0)
            high = zc.astype(BF16)
            low = (zc - high.astype(F32)).astype(BF16)
            done = jnp.dot(qt[s], high, preferred_element_type=F32) + jnp.dot(qt[s], low, preferred_element_type=F32)
            for r in range(2):
                out_ref[s, r, t] = done[192 * r:192 * r + 192]


def body(elemental, peramb_one, peramb_two, gen_peramb):
    dma = pltpu.SemaphoreType.DMA
    vmem = pl.BlockSpec(memory_space=pltpu.VMEM)
    rows = (0, 2, 1, 3)
    out = pl.pallas_call(
        kernel,
        out_shape=jax.ShapeDtypeStruct((2, 2, 3, 192, 192), F32),
        in_specs=[pl.BlockSpec(memory_space=pltpu.HBM)] * 4,
        out_specs=vmem,
        scratch_shapes=[
            pltpu.VMEM((6, 192, 192), BF16),
            pltpu.VMEM((2, 3, 2, 192), BF16),
            pltpu.VMEM((2, 3, 2, 192), BF16),
            pltpu.VMEM((2, 3, 2, 192), BF16),
            pltpu.VMEM((8, 80, 128), BF16),
            pltpu.VMEM((8, 80, 128), BF16),
            pltpu.VMEM((640, 128), F32),
            pltpu.VMEM((64, 128), BF16),
            pltpu.VMEM((8, 64, 128), BF16),
            pltpu.VMEM((512, 128), F32),
            pltpu.VMEM((16, 384), BF16),
            pltpu.VMEM((8, 16, 384), BF16),
            pltpu.VMEM((3, 128, 128), F32),
            pltpu.VMEM((8, 48, 512), BF16),
            pltpu.VMEM((8, 48, 640), BF16),
            pltpu.VMEM((8, 48, 128), BF16),
            pltpu.VMEM((8, 48, 128), BF16),
            pltpu.VMEM((8, 96, 384), BF16),
            pltpu.VMEM((8, 16, 384), BF16),
            pltpu.VMEM((8, 16, 512), BF16),
            pltpu.VMEM((4, 8, 16, 384), BF16),
            pltpu.VMEM((4, 8, 16, 512), BF16),
            pltpu.VMEM((7, 512, 128), F32),
            pltpu.VMEM((512, 128), F32),
            pltpu.VMEM((2, 2, 288, 512), BF16),
            pltpu.VMEM((2, 2, 288, 192), F32),
            pltpu.VMEM((2, 2, 288, 192), F32),
            pltpu.VMEM((2, 384, 384), BF16),
            pltpu.VMEM((2, 2, 2, 512, 192), BF16),
            dma((4,)),
        ] + [dma((8,))] * 18 + [dma((4,))] * 4,
        compiler_params=pltpu.CompilerParams(
            collective_id=0, has_side_effects=True, vmem_limit_bytes=48 << 20),
        name="sink",
    )(*[pltpu.with_memory_space_constraint(a, pltpu.HBM) for a in (
        elemental.reshape(6, 192, 192), jnp.transpose(peramb_one, rows), jnp.transpose(peramb_two, rows),
        jnp.transpose(gen_peramb[0], rows),
    )])
    return out.reshape(1, 1, 2, 2, 3, 192, 192)


def solution(mesh):
    return jax.shard_map(
        body,
        mesh=mesh,
        in_specs=(
            P(None, None, "idx", None, None),
            P("spin", None, "idx", None),
            P("spin", None, "idx", None),
            P("cur", "spin", None, "idx", None),
        ),
        out_specs=P(None, "cur", "spin", None, "idx", None, None),
        check_vma=False,
    )
```

```python
import jax
import jax.numpy as jnp
from jax import lax
from jax.experimental import pallas as pl
from jax.experimental.pallas import tpu as pltpu
from jax.sharding import PartitionSpec as P

MESH = pl.DeviceIdType.MESH
F32, BF16 = jnp.float32, jnp.bfloat16
TN = (((0,), (0,)), ((), ()))
POWER = 32768.0
RELAY_V = True
RELAY_X = True
FAR_FIRST = (4, 3, 5, 2, 6, 1, 7)
SLOT = {1: 2, 2: 3, 3: 1}


def kernel(
    e_hbm, p_hbm, q_hbm, g_hbm, out_ref,
    e_ref, p_ref, q_ref, g_ref, e0, e1, ef, p0, p1, pf, qg0, qg1, qf,
    eba, ebb, psend, pbuf, qgbuf, xsa, xsb, xba, xbb, xf, xr, ah, zr, zi, qt, gw,
    in_sem, e1s, e1r, p1s, p1r, q1s, q1r, eas, ear, ebs, ebr, p2s, p2r, q2s, q2r,
    xas, xar, xbs, xbr, fas, far, fbs, fbr,
):
    idx, x, k = lax.axis_index("idx"), lax.axis_index("cur"), lax.axis_index("spin")
    y, z = idx // 8, idx % 8
    u = y * (1 - k) + z * k
    v = z * (1 - k) + y * k

    def column(uu, vv):
        return (uu * (1 - k) + vv * k) * 8 + vv * (1 - k) + uu * k

    def on_u(d):
        return (u + d) % 8

    def on_v(d):
        return (v + d) % 8

    def send(src, dst, ss, rs, where):
        copy = pltpu.make_async_remote_copy(
            src_ref=src, dst_ref=dst, send_sem=ss, recv_sem=rs, device_id=where, device_id_type=MESH
        )
        copy.start()
        return copy

    def to_u(d):
        return column(on_u(d), v), x, k

    def to_v(d):
        return column(u, on_v(d)), x, k

    loads = [
        pltpu.make_async_copy(src, dst, in_sem.at[i])
        for i, (src, dst) in enumerate(((e_hbm, e_ref), (p_hbm, p_ref), (q_hbm, q_ref), (g_hbm, g_ref)))
    ]
    for c in loads:
        c.start()
    barrier = pltpu.get_barrier_semaphore()
    for d in FAR_FIRST:
        pl.semaphore_signal(barrier, inc=1, device_id=to_u(d), device_id_type=MESH)
        pl.semaphore_signal(barrier, inc=1, device_id=to_v(d), device_id_type=MESH)
    for d in (2, 1, 3):
        pl.semaphore_signal(barrier, inc=1, device_id=(idx, (x + d) % 4, k), device_id_type=MESH)

    row = lax.broadcasted_iota(jnp.int32, (64, 1), 0)
    uu, beta = row >> 3, row & 7
    h = jnp.where(beta >= 3, 1, 0)
    t = beta - 3 * h
    source = 24 * (uu * (1 - k) + (2 * x + h) * k) + 3 * ((2 * x + h) * (1 - k) + uu * k) + t
    source = jnp.where(beta < 6, source, -1)
    pick_e = jnp.where(source == lax.broadcasted_iota(jnp.int32, (64, 192), 1), 1.0, 0.0).astype(BF16)
    n = lax.broadcasted_iota(jnp.int32, (1, 1024), 1)
    nv, nu, nt = n >> 7, (n >> 4) & 7, (n >> 2) & 3
    owner = 8 * (nu * (1 - k) + nv * k) + nv * (1 - k) + nu * k
    column_of = jnp.where((nt < 3) & ((n & 3) == 0), 3 * owner + nt, -1)
    pick_p = jnp.where(column_of == lax.broadcasted_iota(jnp.int32, (192, 1024), 0), 1.0, 0.0).astype(BF16)
    loads[0].wait()
    picked = [jnp.dot(pick_e, e_ref[i], preferred_element_type=F32) for i in range(6)]
    e0[...] = jnp.concatenate(
        [m[:, :128].reshape(8, 8, 128) for m in picked]
        + [
            jnp.concatenate([picked[2 * i][:, 128:], picked[2 * i + 1][:, 128:]], axis=1).reshape(8, 8, 128)
            for i in range(3)
        ]
        + [jnp.zeros((8, 8, 128), F32)], axis=1).astype(BF16)
    pl.semaphore_wait(barrier, 17)

    e_sends = [send(e0.at[on_u(d)], e1.at[u], e1s.at[d - 1], e1r.at[d - 1], to_u(d)) for d in FAR_FIRST]
    for c in loads[1:]:
        c.wait()
    p = p_ref[...].astype(F32)
    p = jnp.concatenate([p[s, :, r, :] for s in range(2) for r in range(2)], axis=0)
    spread = jnp.dot(p.astype(BF16), pick_p, preferred_element_type=F32)
    by = [spread] + [pltpu.roll(spread, i, 1) for i in range(1, 4)]
    upper = by[0][0:3] + by[1][3:6] + by[2][6:9] + by[3][9:12]
    lower = by[1][0:3] - by[0][3:6] + by[3][6:9] - by[2][9:12]
    both = jnp.concatenate([upper, lower, jnp.zeros((2, 1024), F32)], axis=0)
    p0[...] = jnp.concatenate([both[:, 128 * i:128 * i + 128] for i in range(8)], axis=0).astype(BF16)
    qg0[...] = jnp.concatenate([
        jnp.concatenate([a[s, :, r, :] for s in range(2) for r in range(2)] + [jnp.zeros((4, 192), F32)], axis=0)
        for a in (q_ref[...].astype(F32), g_ref[...].astype(F32))
    ], axis=1).astype(BF16)
    p_sends = [send(p0, p1.at[u], p1s.at[d - 1], p1r.at[d - 1], to_u(d)) for d in FAR_FIRST]
    e1[u] = e0[u]
    p1[u] = p0[...]
    qg1[u] = qg0[...]

    left = lax.broadcasted_iota(jnp.int32, (8, 128), 1) < 64

    def tile(m):
        j, m = m // 3, m % 3
        pieces = []
        for i in range(6):
            if m < 2:
                pieces.append(ef[pl.ds(8 * i + 2 * j + m, 8, stride=80), :])
                continue
            first, second = [ef[pl.ds(48 + 8 * (i // 2) + 2 * j + b, 8, stride=80), :] for b in range(2)]
            if i % 2 == 0:
                second = pltpu.roll(second, 64, 1)
            else:
                first = pltpu.roll(first, 64, 1)
            pieces.append(jnp.where(left, first, second))
        return jnp.concatenate(pieces, axis=0).astype(BF16)

    for c in e_sends:
        c.wait()
    ef[...] = e1[...].astype(F32).reshape(640, 128)
    for m in range(4):
        eba[v, :, pl.ds(128 * m, 128)] = tile(m)
    def first_leg(block, ss, rs):
        return {
            d: send(block.at[v], block.at[v], ss.at[d - 1], rs.at[d - 1], to_v(d))
            for d in ((2, 6, 1, 7) if RELAY_V else FAR_FIRST)
        }

    def second_leg(block, cut, sent, ss, rs):
        if not RELAY_V:
            return []
        size = block.shape[2]
        more = []
        for d, near, lanes, place in ((2, 1, pl.ds(0, cut), 3), (6, 7, pl.ds(cut, size - cut), 7)):
            sent[d].wait()
            came = (v - d + 8) % 8
            whole, part = block.at[came], block.at[came, :, lanes]
            more.append(send(whole, whole, ss.at[2 if d == 2 else 4], rs.at[2 if d == 2 else 4], to_v(near)))
            more.append(send(part, part, ss.at[place], rs.at[place], to_v(d)))
        return [sent[1], sent[7]] + more

    a_sent = first_leg(eba, eas, ear)
    for c in p_sends:
        c.wait()
    pf[...] = p1[...].astype(F32).reshape(512, 128)
    for i in range(8):
        psend[i] = jnp.concatenate(
            [pf[pl.ds(8 * i + r, 8, stride=64), :] for r in range(6)], axis=0).astype(BF16)
    a_sends = [send(psend.at[on_v(d)], pbuf.at[v], p2s.at[d - 1], p2r.at[d - 1], to_v(d)) for d in FAR_FIRST]
    pbuf[v] = psend[v]
    for m in range(5):
        ebb[v, :, pl.ds(128 * m, 128)] = tile(4 + m)
    b_sent = first_leg(ebb, ebs, ebr)
    q_sends = [send(qg0, qg1.at[u], q1s.at[d - 1], q1r.at[d - 1], to_u(d)) for d in FAR_FIRST]
    if RELAY_V:
        a_sends += second_leg(eba, 256, a_sent, eas, ear)
        b_sends = second_leg(ebb, 384, b_sent, ebs, ebr)
    else:
        a_sends += list(a_sent.values())
        b_sends = list(b_sent.values())

    weights = None

    def contract(part, tiles):
        value = lax.dot_general(weights, part[...].reshape(384, 128 * tiles), TN, preferred_element_type=F32)
        largest = jnp.maximum(jnp.max(jnp.abs(value)), 1e-30)
        largest = jnp.full((8, 8, 128), largest, F32).astype(BF16).astype(F32)
        halves = []
        for m in range(tiles):
            scaled = value[:, 128 * m:128 * m + 128].reshape(8, 2, 8, 128)
            pair = []
            for i in range(2):
                a = scaled[:, i] * (POWER / largest)
                square = a * a
                fourth = square * square
                pair.append(jnp.where(a < 0, -fourth, fourth) * fourth)
            halves.append(pair)
        return halves, largest

    def along_x(block, there, here, part, sem, ss, rs, s):
        return send(block.at[here, part], block.at[there, part], ss.at[sem], rs.at[sem], (idx, (x + s) % 4, k))

    def spread_x(block, ss, rs):
        return {
            s: along_x(block, SLOT[s], 0, pl.ds(0, 8), s - 1, ss, rs, s) for s in ((1, 3) if RELAY_X else (2, 1, 3))
        }

    def pass_x(block, sent, ss, rs):
        for s in (1, 3):
            sent[s].wait()
        if not RELAY_X:
            return [sent[2]]
        return [
            along_x(block, 3, 2, pl.ds(0, 4), 1, ss, rs, 1), along_x(block, 3, 1, pl.ds(4, 4), 3, ss, rs, 3)
        ]

    def decode(i):
        for m in range(7):
            code = (xba[i, :, :, 128 * m:128 * m + 128] if m < 3 else xbb[i, :, :, 128 * m - 384:128 * m - 256])
            code = code.astype(F32).reshape(128, 128)
            if m == 6:
                xr[pl.ds(128 * i, 128)] = code
            root = lax.rsqrt(jnp.maximum(jnp.abs(code), 1.2e-38))
            fourth = lax.rsqrt(root)
            size = fourth * lax.rsqrt(fourth)
            xf[m, pl.ds(128 * i, 128)] = jnp.where(code < 0, -size, size)

    low_rows = lax.broadcasted_iota(jnp.int32, (8, 8, 128), 1) < 4

    def third(pair, t):
        return pair[0] if t == 1 else pltpu.roll(pair[t // 2], 4, 1)

    def put(dst, m, first, second):
        dst[:, :, 128 * m:128 * m + 128] = jnp.concatenate([first, second], axis=1).astype(BF16)

    for c in a_sends:
        c.wait()
    weights = pbuf[...].reshape(384, 128)
    halves, scale_a = contract(eba, 4)
    for m in range(3):
        put(xsa, m, halves[m][0], jnp.where(low_rows, halves[m][1], third(halves[3], m)))
    xa_sends = [
        send(xsa.at[on_u(d)], xba.at[0, u], xas.at[d - 1], xar.at[d - 1], to_u(d)) for d in FAR_FIRST
    ]
    xba[0, u] = xsa[u]
    for c in b_sends:
        c.wait()
    halves, scale_b = contract(ebb, 5)
    for m in range(3):
        put(xsb, m, halves[m][0], jnp.where(low_rows, halves[m][1], third(halves[4], m)))
    sub = lax.broadcasted_iota(jnp.int32, (8, 8, 128), 1)
    put(xsb, 3, halves[3][0], jnp.where(low_rows, halves[3][1], jnp.where(sub == 4, scale_a, scale_b)))
    xb_sends = [
        send(xsb.at[on_u(d)], xbb.at[0, u], xbs.at[d - 1], xbr.at[d - 1], to_u(d)) for d in FAR_FIRST
    ]
    xbb[0, u] = xsb[u]

    for c in q_sends:
        c.wait()
    for i in range(3):
        qf[i] = qg1[:, :, 128 * i:128 * i + 128].astype(F32).reshape(128, 128)
        qgbuf[v, :, pl.ds(128 * i, 128)] = jnp.concatenate(
            [qf[i, pl.ds(r, 8, stride=16), :] for r in range(12)], axis=0).astype(BF16)
    qg_sent = first_leg(qgbuf, q2s, q2r)
    for c in xa_sends:
        c.wait()
    fa_sends = spread_x(xba, fas, far)
    qg_sends = second_leg(qgbuf, 256, qg_sent, q2s, q2r)
    for c in xb_sends:
        c.wait()
    fb_sends = spread_x(xbb, fbs, fbr)
    fa_more = pass_x(xba, fa_sends, fas, far)
    fb_more = pass_x(xbb, fb_sends, fbs, fbr)
    for i in (0, 1, 2):
        decode(i)
    received = lax.broadcasted_iota(jnp.int32, (192, 1), 0)
    wanted = lax.broadcasted_iota(jnp.int32, (192, 192), 1)
    rv, rt, ru = received // 24, received // 8 % 3, received % 8
    natural = rt + 3 * (rv * (1 - k) + ru * k) + 24 * (ru * (1 - k) + rv * k)
    place_g = jnp.where(natural == wanted, 1.0, 0.0).astype(BF16)
    beta = 3 * (rv % 2) + rt
    ahead = (rv // 2 - x + 4) % 4
    slot = jnp.where(ahead < 2, ahead, 5 - ahead)
    order = (beta % 2) * 96 + (slot // 2) * 48 + (beta // 2) * 16 + (slot % 2) * 8 + ru
    place_q = jnp.where(order == wanted, 1.0, 0.0).astype(BF16)
    none = jnp.zeros((64, 192), BF16)
    gw[:, :, :, 128:256] = jnp.zeros((2, 2, 512, 128), BF16)
    for c in qg_sends:
        c.wait()

    for s in range(2):
        qs, gs = [], []
        for r in range(2):
            part = jnp.concatenate(
                [qgbuf[i, pl.ds(48 * s + 24 * r, 24), :].astype(F32) for i in range(8)], axis=0).astype(BF16)
            qs.append(lax.dot_general(part[:, :192], place_q, TN, preferred_element_type=F32).astype(BF16))
            gs.append(lax.dot_general(place_g, part[:, 192:], TN, preferred_element_type=F32).astype(BF16))
        qr, qi = qs
        for i in (0, 384):
            qt[s, :192, i:i + 192], qt[s, :192, i + 192:i + 384] = qr, -qi
            qt[s, 192:, i:i + 192], qt[s, 192:, i + 192:i + 384] = qi, qr
        for odd in range(2):
            gr, gi = [
                jnp.concatenate([m[:128], none, m[128:]] if odd else [m, none], axis=0) for m in gs
            ]
            gw[s, odd, :256, :192], gw[s, odd, 256:, :192] = gr, -gi
            gw[s, odd, :256, 256:], gw[s, odd, 256:, 256:] = gi, gr

    for half in range(2):
        if half == 1:
            for c in fa_more + fb_more:
                c.wait()
            decode(3)
        scales = [xr[pl.ds(256 * half + 12 + i, 16, stride=16), :] * (1.0 / POWER) for i in range(2)]
        for s in range(2):
            for t in range(3):
                for r in range(2):
                    for m in range(9):
                        if m in (3, 8):
                            place, row = t if m == 3 else 3 + t, 12 + 2 * s + r
                        else:
                            place, row = m if m < 3 else m - 1, 4 * t + 2 * s + r
                        j, kind = m // 3, m % 3
                        code = xf[place, pl.ds(256 * half + row, 16, stride=16), :]
                        value = code * scales[0 if m < 4 else 1]
                        high = value.astype(BF16)
                        low = (value - high.astype(F32)).astype(BF16)
                        at = pl.ds(48 * t + 16 * j, 16)
                        for odd in range(2):
                            if kind in (odd, 2):
                                lane = pl.ds(256 * r + (128 if kind == 2 else 0), 128)
                                ah[s, odd, at, lane] = high
                                ah[s, odd, pl.ds(144 + 48 * t + 16 * j, 16), lane] = low
        for s in range(2):
            for odd in range(2):
                both = jnp.dot(ah[s, odd], gw[s, odd], preferred_element_type=F32)
                both = both[:144] + both[144:]
                zr[s, odd, pl.ds(144 * half, 144)] = both[:, :192]
                zi[s, odd, pl.ds(144 * half, 144)] = both[:, 256:]

    for s in range(2):
        for t in range(3):
            zc = jnp.concatenate([
                m[s, odd, pl.ds(144 * half + 48 * t, 48)] for m in (zr, zi) for odd in range(2) for half in range(2)
            ], axis=0)
            high = zc.astype(BF16)
            low = (zc - high.astype(F32)).astype(BF16)
            done = jnp.dot(qt[s], jnp.concatenate([high, low], axis=0), preferred_element_type=F32)
            for r in range(2):
                out_ref[s, r, t] = done[192 * r:192 * r + 192]


def body(elemental, peramb_one, peramb_two, gen_peramb):
    dma = pltpu.SemaphoreType.DMA
    vmem = pl.BlockSpec(memory_space=pltpu.VMEM)
    rows = (0, 2, 1, 3)
    out = pl.pallas_call(
        kernel,
        out_shape=jax.ShapeDtypeStruct((2, 2, 3, 192, 192), F32),
        in_specs=[pl.BlockSpec(memory_space=pltpu.HBM)] * 4,
        out_specs=vmem,
        scratch_shapes=[
            pltpu.VMEM((6, 192, 192), BF16),
            pltpu.VMEM((2, 3, 2, 192), BF16),
            pltpu.VMEM((2, 3, 2, 192), BF16),
            pltpu.VMEM((2, 3, 2, 192), BF16),
            pltpu.VMEM((8, 80, 128), BF16),
            pltpu.VMEM((8, 80, 128), BF16),
            pltpu.VMEM((640, 128), F32),
            pltpu.VMEM((64, 128), BF16),
            pltpu.VMEM((8, 64, 128), BF16),
            pltpu.VMEM((512, 128), F32),
            pltpu.VMEM((16, 384), BF16),
            pltpu.VMEM((8, 16, 384), BF16),
            pltpu.VMEM((3, 128, 128), F32),
            pltpu.VMEM((8, 48, 512), BF16),
            pltpu.VMEM((8, 48, 640), BF16),
            pltpu.VMEM((8, 48, 128), BF16),
            pltpu.VMEM((8, 48, 128), BF16),
            pltpu.VMEM((8, 96, 384), BF16),
            pltpu.VMEM((8, 16, 384), BF16),
            pltpu.VMEM((8, 16, 512), BF16),
            pltpu.VMEM((4, 8, 16, 384), BF16),
            pltpu.VMEM((4, 8, 16, 512), BF16),
            pltpu.VMEM((7, 512, 128), F32),
            pltpu.VMEM((512, 128), F32),
            pltpu.VMEM((2, 2, 288, 512), BF16),
            pltpu.VMEM((2, 2, 288, 192), F32),
            pltpu.VMEM((2, 2, 288, 192), F32),
            pltpu.VMEM((2, 384, 768), BF16),
            pltpu.VMEM((2, 2, 512, 448), BF16),
            dma((4,)),
        ] + [dma((8,))] * 18 + [dma((4,))] * 4,
        compiler_params=pltpu.CompilerParams(
            collective_id=0, has_side_effects=True, vmem_limit_bytes=48 << 20),
        name="sink",
    )(*[pltpu.with_memory_space_constraint(a, pltpu.HBM) for a in (
        elemental.reshape(6, 192, 192), jnp.transpose(peramb_one, rows), jnp.transpose(peramb_two, rows),
        jnp.transpose(gen_peramb[0], rows),
    )])
    return out.reshape(1, 1, 2, 2, 3, 192, 192)


def solution(mesh):
    return jax.shard_map(
        body,
        mesh=mesh,
        in_specs=(
            P(None, None, "idx", None, None),
            P("spin", None, "idx", None),
            P("spin", None, "idx", None),
            P("cur", "spin", None, "idx", None),
        ),
        out_specs=P(None, "cur", "spin", None, "idx", None, None),
        check_vma=False,
    )
```

```python
import jax
import jax.numpy as jnp
from jax import lax
from jax.experimental import pallas as pl
from jax.experimental.pallas import tpu as pltpu
from jax.sharding import PartitionSpec as P

MESH = pl.DeviceIdType.MESH
F32, BF16 = jnp.float32, jnp.bfloat16
TN = (((0,), (0,)), ((), ()))
POWER = 32768.0
RELAY_V = True
RELAY_X = True
FAR_FIRST = (4, 3, 5, 2, 6, 1, 7)
SLOT = {1: 2, 2: 3, 3: 1}


def kernel(
    e_hbm, p_hbm, q_hbm, g_hbm, out_ref,
    e_ref, p_ref, q_ref, g_ref, e0, e1, ef, sel, qg0, qg1, qf,
    eba, ebb, psend, pbuf, qgbuf, xsa, xsb, xba, xbb, xf, xr, ah, zr, zi, qt, gw,
    in_sem, e1s, e1r, q1s, q1r, eas, ear, ebs, ebr, p2s, p2r, q2s, q2r,
    xas, xar, xbs, xbr, fas, far, fbs, fbr,
):
    idx, x, k = lax.axis_index("idx"), lax.axis_index("cur"), lax.axis_index("spin")
    y, z = idx // 8, idx % 8
    u = y * (1 - k) + z * k
    v = z * (1 - k) + y * k

    def column(uu, vv):
        return (uu * (1 - k) + vv * k) * 8 + vv * (1 - k) + uu * k

    def on_u(d):
        return (u + d) % 8

    def on_v(d):
        return (v + d) % 8

    started = []

    def send(src, dst, ss, rs, where):
        copy = pltpu.make_async_remote_copy(
            src_ref=src, dst_ref=dst, send_sem=ss, recv_sem=rs, device_id=where, device_id_type=MESH
        )
        copy.start()
        started.append(copy)
        return copy

    def to_u(d):
        return column(on_u(d), v), x, k

    def to_v(d):
        return column(u, on_v(d)), x, k

    loads = [
        pltpu.make_async_copy(src, dst, in_sem.at[i])
        for i, (src, dst) in enumerate(
            [(e_hbm.at[i], e_ref.at[i]) for i in range(6)] + [(p_hbm, p_ref), (q_hbm, q_ref), (g_hbm, g_ref)])
    ]
    for c in loads:
        c.start()
    barrier = pltpu.get_barrier_semaphore()
    for d in FAR_FIRST:
        pl.semaphore_signal(barrier, inc=1, device_id=to_u(d), device_id_type=MESH)
        pl.semaphore_signal(barrier, inc=1, device_id=to_v(d), device_id_type=MESH)
    for d in (2, 1, 3):
        pl.semaphore_signal(barrier, inc=1, device_id=(idx, (x + d) % 4, k), device_id_type=MESH)

    row = lax.broadcasted_iota(jnp.int32, (64, 1), 0)
    uu, beta = row >> 3, row & 7
    h = jnp.where(beta >= 3, 1, 0)
    t = beta - 3 * h
    source = 24 * (uu * (1 - k) + (2 * x + h) * k) + 3 * ((2 * x + h) * (1 - k) + uu * k) + t
    source = jnp.where(beta < 6, source, -1)
    pick_e = jnp.where(source == lax.broadcasted_iota(jnp.int32, (64, 192), 1), 1.0, 0.0).astype(BF16)
    loads[6].wait()
    p = p_ref[...].astype(F32)
    place = lax.broadcasted_iota(jnp.int32, (64, 192), 0) & 7
    picked = []
    for i in range(6):
        loads[i].wait()
        rows = jnp.dot(pick_e, e_ref[i], preferred_element_type=F32)
        for s in range(2):
            rows = jnp.where(place == 6 + s, p[s, i // 2, i % 2:i % 2 + 1, :], rows)
        picked.append(rows)
    e0[...] = jnp.concatenate(
        [m[:, :128].reshape(8, 8, 128) for m in picked]
        + [
            jnp.concatenate([picked[2 * i][:, 128:], picked[2 * i + 1][:, 128:]], axis=1).reshape(8, 8, 128)
            for i in range(3)
        ]
        + [jnp.zeros((8, 8, 128), F32)], axis=1).astype(BF16)
    pl.semaphore_wait(barrier, 17)

    e_sends = [send(e0.at[on_u(d)], e1.at[u], e1s.at[d - 1], e1r.at[d - 1], to_u(d)) for d in FAR_FIRST]
    for c in loads[7:]:
        c.wait()
    qg0[...] = jnp.concatenate([
        jnp.concatenate([a[s, :, r, :] for s in range(2) for r in range(2)] + [jnp.zeros((4, 192), F32)], axis=0)
        for a in (q_ref[...].astype(F32), g_ref[...].astype(F32))
    ], axis=1).astype(BF16)
    e1[u] = e0[u]
    qg1[u] = qg0[...]
    q_sends = [send(qg0, qg1.at[u], q1s.at[d - 1], q1r.at[d - 1], to_u(d)) for d in FAR_FIRST]
    n = lax.broadcasted_iota(jnp.int32, (1, 1024), 1)
    nv, nu, nt = n >> 7, (n >> 4) & 7, (n >> 2) & 3
    owner = 8 * (nu * (1 - k) + nv * k) + nv * (1 - k) + nu * k
    wanted = jnp.where(nt < 3, 3 * owner + nt + 192 * (n & 3), -1)
    at = lax.broadcasted_iota(jnp.int32, (128, 1), 0)
    for i in range(6):
        if i < 4:
            key = 192 * i + at
        else:
            key = 192 * (2 * (i - 4) + (at >> 6)) + 128 + (at & 63)
        sel[128 * i:128 * i + 128, :] = jnp.where(key == wanted, 1.0, 0.0).astype(BF16)

    left = lax.broadcasted_iota(jnp.int32, (8, 128), 1) < 64

    def tile(m):
        j, m = m // 3, m % 3
        pieces = []
        for i in range(6):
            if m < 2:
                pieces.append(ef[pl.ds(8 * i + 2 * j + m, 8, stride=80), :])
                continue
            first, second = [ef[pl.ds(48 + 8 * (i // 2) + 2 * j + b, 8, stride=80), :] for b in range(2)]
            if i % 2 == 0:
                second = pltpu.roll(second, 64, 1)
            else:
                first = pltpu.roll(first, 64, 1)
            pieces.append(jnp.where(left, first, second))
        return jnp.concatenate(pieces, axis=0).astype(BF16)

    for c in e_sends:
        c.wait_recv()
    ef[...] = e1[...].astype(F32).reshape(640, 128)
    for m in range(4):
        eba[v, :, pl.ds(128 * m, 128)] = tile(m)
    def first_leg(block, ss, rs):
        return {
            d: send(block.at[v], block.at[v], ss.at[d - 1], rs.at[d - 1], to_v(d))
            for d in ((2, 6, 1, 7) if RELAY_V else FAR_FIRST)
        }

    def second_leg(block, cut, sent, ss, rs):
        if not RELAY_V:
            return []
        size = block.shape[2]
        more = []
        for d, near, lanes, place in ((2, 1, pl.ds(0, cut), 3), (6, 7, pl.ds(cut, size - cut), 7)):
            sent[d].wait_recv()
            came = (v - d + 8) % 8
            whole, part = block.at[came], block.at[came, :, lanes]
            more.append(send(whole, whole, ss.at[2 if d == 2 else 4], rs.at[2 if d == 2 else 4], to_v(near)))
            more.append(send(part, part, ss.at[place], rs.at[place], to_v(d)))
        return [sent[1], sent[7]] + more

    a_sent = first_leg(eba, eas, ear)
    lhs = []
    for r in range(2):
        for i in range(3):
            tiles = []
            for s in range(2):
                pr, pi = [ef[pl.ds(8 * (2 * i + c) + 6 + s, 8, stride=80), :] for c in range(2)]
                tiles += [pr, pi] if r == 0 else [-pi, pr]
            for s in range(2):
                both = ef[pl.ds(48 + 8 * i + 6 + s, 8, stride=80), :]
                if r == 1:
                    both = pltpu.roll(both, 64, 1)
                    both = jnp.where(left, -both, both)
                tiles.append(both)
            lhs.append(jnp.concatenate(tiles, axis=1))
    chosen = jnp.dot(jnp.concatenate(lhs, axis=0).astype(BF16), sel[...], preferred_element_type=F32).astype(BF16)
    for i in range(8):
        psend[i] = chosen[:, 128 * i:128 * i + 128]
    a_sends = [send(psend.at[on_v(d)], pbuf.at[v], p2s.at[d - 1], p2r.at[d - 1], to_v(d)) for d in FAR_FIRST]
    pbuf[v] = psend[v]
    for m in range(5):
        ebb[v, :, pl.ds(128 * m, 128)] = tile(4 + m)
    b_sent = first_leg(ebb, ebs, ebr)
    if RELAY_V:
        a_sends += second_leg(eba, 256, a_sent, eas, ear)
        b_sends = second_leg(ebb, 384, b_sent, ebs, ebr)
    else:
        a_sends += list(a_sent.values())
        b_sends = list(b_sent.values())

    weights = None

    def contract(part, tiles):
        value = lax.dot_general(weights, part[...].reshape(384, 128 * tiles), TN, preferred_element_type=F32)
        largest = jnp.maximum(jnp.max(jnp.abs(value)), 1e-30)
        largest = jnp.full((8, 8, 128), largest, F32).astype(BF16).astype(F32)
        halves = []
        for m in range(tiles):
            scaled = value[:, 128 * m:128 * m + 128].reshape(8, 2, 8, 128)
            pair = []
            for i in range(2):
                a = scaled[:, i] * (POWER / largest)
                square = a * a
                fourth = square * square
                pair.append(jnp.where(a < 0, -fourth, fourth) * fourth)
            halves.append(pair)
        return halves, largest

    def along_x(block, there, here, part, sem, ss, rs, s):
        return send(block.at[here, part], block.at[there, part], ss.at[sem], rs.at[sem], (idx, (x + s) % 4, k))

    def spread_x(block, ss, rs):
        return {
            s: along_x(block, SLOT[s], 0, pl.ds(0, 8), s - 1, ss, rs, s) for s in ((1, 3) if RELAY_X else (2, 1, 3))
        }

    def pass_x(block, sent, ss, rs):
        for s in (1, 3):
            sent[s].wait_recv()
        if not RELAY_X:
            return [sent[2]]
        return [
            along_x(block, 3, 2, pl.ds(0, 4), 1, ss, rs, 1), along_x(block, 3, 1, pl.ds(4, 4), 3, ss, rs, 3)
        ]

    def decode(i):
        for m in range(7):
            code = (xba[i, :, :, 128 * m:128 * m + 128] if m < 3 else xbb[i, :, :, 128 * m - 384:128 * m - 256])
            code = code.astype(F32).reshape(128, 128)
            if m == 6:
                xr[pl.ds(128 * i, 128)] = code
            root = lax.rsqrt(jnp.maximum(jnp.abs(code), 1.2e-38))
            fourth = lax.rsqrt(root)
            size = fourth * lax.rsqrt(fourth)
            xf[m, pl.ds(128 * i, 128)] = jnp.where(code < 0, -size, size)

    low_rows = lax.broadcasted_iota(jnp.int32, (8, 8, 128), 1) < 4

    def third(pair, t):
        return pair[0] if t == 1 else pltpu.roll(pair[t // 2], 4, 1)

    def put(dst, m, first, second):
        dst[:, :, 128 * m:128 * m + 128] = jnp.concatenate([first, second], axis=1).astype(BF16)

    for c in a_sends:
        c.wait_recv()
    weights = pbuf[...].reshape(384, 128)
    halves, scale_a = contract(eba, 4)
    for m in range(3):
        put(xsa, m, halves[m][0], jnp.where(low_rows, halves[m][1], third(halves[3], m)))
    xa_sends = [
        send(xsa.at[on_u(d)], xba.at[0, u], xas.at[d - 1], xar.at[d - 1], to_u(d)) for d in FAR_FIRST
    ]
    xba[0, u] = xsa[u]
    for c in b_sends:
        c.wait_recv()
    halves, scale_b = contract(ebb, 5)
    for m in range(3):
        put(xsb, m, halves[m][0], jnp.where(low_rows, halves[m][1], third(halves[4], m)))
    sub = lax.broadcasted_iota(jnp.int32, (8, 8, 128), 1)
    put(xsb, 3, halves[3][0], jnp.where(low_rows, halves[3][1], jnp.where(sub == 4, scale_a, scale_b)))
    xb_sends = [
        send(xsb.at[on_u(d)], xbb.at[0, u], xbs.at[d - 1], xbr.at[d - 1], to_u(d)) for d in FAR_FIRST
    ]
    xbb[0, u] = xsb[u]

    for c in q_sends:
        c.wait_recv()
    for i in range(3):
        qf[i] = qg1[:, :, 128 * i:128 * i + 128].astype(F32).reshape(128, 128)
        qgbuf[v, :, pl.ds(128 * i, 128)] = jnp.concatenate(
            [qf[i, pl.ds(r, 8, stride=16), :] for r in range(12)], axis=0).astype(BF16)
    qg_sent = first_leg(qgbuf, q2s, q2r)
    for c in xa_sends:
        c.wait_recv()
    fa_sends = spread_x(xba, fas, far)
    qg_sends = second_leg(qgbuf, 256, qg_sent, q2s, q2r)
    for c in xb_sends:
        c.wait_recv()
    fb_sends = spread_x(xbb, fbs, fbr)
    fa_more = pass_x(xba, fa_sends, fas, far)
    fb_more = pass_x(xbb, fb_sends, fbs, fbr)
    for i in (0, 1, 2):
        decode(i)
    received = lax.broadcasted_iota(jnp.int32, (192, 1), 0)
    wanted = lax.broadcasted_iota(jnp.int32, (192, 192), 1)
    rv, rt, ru = received // 24, received // 8 % 3, received % 8
    natural = rt + 3 * (rv * (1 - k) + ru * k) + 24 * (ru * (1 - k) + rv * k)
    place_g = jnp.where(natural == wanted, 1.0, 0.0).astype(BF16)
    beta = 3 * (rv % 2) + rt
    ahead = (rv // 2 - x + 4) % 4
    slot = jnp.where(ahead < 2, ahead, 5 - ahead)
    order = (beta % 2) * 96 + (slot // 2) * 48 + (beta // 2) * 16 + (slot % 2) * 8 + ru
    place_q = jnp.where(order == wanted, 1.0, 0.0).astype(BF16)
    none = jnp.zeros((64, 192), BF16)
    gw[:, :, :, 128:256] = jnp.zeros((2, 2, 512, 128), BF16)
    for c in qg_sends:
        c.wait_recv()

    for s in range(2):
        qs, gs = [], []
        for r in range(2):
            part = jnp.concatenate(
                [qgbuf[i, pl.ds(48 * s + 24 * r, 24), :].astype(F32) for i in range(8)], axis=0).astype(BF16)
            qs.append(lax.dot_general(part[:, :192], place_q, TN, preferred_element_type=F32).astype(BF16))
            gs.append(lax.dot_general(place_g, part[:, 192:], TN, preferred_element_type=F32).astype(BF16))
        qr, qi = qs
        for i in (0, 384):
            qt[s, :192, i:i + 192], qt[s, :192, i + 192:i + 384] = qr, -qi
            qt[s, 192:, i:i + 192], qt[s, 192:, i + 192:i + 384] = qi, qr
        for odd in range(2):
            gr, gi = [
                jnp.concatenate([m[:128], none, m[128:]] if odd else [m, none], axis=0) for m in gs
            ]
            gw[s, odd, :256, :192], gw[s, odd, 256:, :192] = gr, -gi
            gw[s, odd, :256, 256:], gw[s, odd, 256:, 256:] = gi, gr

    for half in range(2):
        if half == 1:
            for c in fa_more + fb_more:
                c.wait_recv()
            decode(3)
        scales = [xr[pl.ds(256 * half + 12 + i, 16, stride=16), :] * (1.0 / POWER) for i in range(2)]
        for s in range(2):
            for t in range(3):
                for r in range(2):
                    for m in range(9):
                        if m in (3, 8):
                            place, row = t if m == 3 else 3 + t, 12 + 2 * s + r
                        else:
                            place, row = m if m < 3 else m - 1, 4 * t + 2 * s + r
                        j, kind = m // 3, m % 3
                        code = xf[place, pl.ds(256 * half + row, 16, stride=16), :]
                        value = code * scales[0 if m < 4 else 1]
                        high = value.astype(BF16)
                        low = (value - high.astype(F32)).astype(BF16)
                        at = pl.ds(48 * t + 16 * j, 16)
                        for odd in range(2):
                            if kind in (odd, 2):
                                lane = pl.ds(256 * r + (128 if kind == 2 else 0), 128)
                                ah[s, odd, at, lane] = high
                                ah[s, odd, pl.ds(144 + 48 * t + 16 * j, 16), lane] = low
        for s in range(2):
            for odd in range(2):
                both = jnp.dot(ah[s, odd], gw[s, odd], preferred_element_type=F32)
                both = both[:144] + both[144:]
                zr[s, odd, pl.ds(144 * half, 144)] = both[:, :192]
                zi[s, odd, pl.ds(144 * half, 144)] = both[:, 256:]

    for s in range(2):
        for t in range(3):
            zc = jnp.concatenate([
                m[s, odd, pl.ds(144 * half + 48 * t, 48)] for m in (zr, zi) for odd in range(2) for half in range(2)
            ], axis=0)
            high = zc.astype(BF16)
            low = (zc - high.astype(F32)).astype(BF16)
            done = jnp.dot(qt[s], jnp.concatenate([high, low], axis=0), preferred_element_type=F32)
            for r in range(2):
                out_ref[s, r, t] = done[192 * r:192 * r + 192]
    for c in started:
        c.wait_send()


def body(elemental, peramb_one, peramb_two, gen_peramb):
    dma = pltpu.SemaphoreType.DMA
    vmem = pl.BlockSpec(memory_space=pltpu.VMEM)
    rows = (0, 2, 1, 3)
    out = pl.pallas_call(
        kernel,
        out_shape=jax.ShapeDtypeStruct((2, 2, 3, 192, 192), F32),
        in_specs=[pl.BlockSpec(memory_space=pltpu.HBM)] * 4,
        out_specs=vmem,
        scratch_shapes=[
            pltpu.VMEM((6, 192, 192), BF16),
            pltpu.VMEM((2, 3, 2, 192), BF16),
            pltpu.VMEM((2, 3, 2, 192), BF16),
            pltpu.VMEM((2, 3, 2, 192), BF16),
            pltpu.VMEM((8, 80, 128), BF16),
            pltpu.VMEM((8, 80, 128), BF16),
            pltpu.VMEM((640, 128), F32),
            pltpu.VMEM((768, 1024), BF16),
            pltpu.VMEM((16, 384), BF16),
            pltpu.VMEM((8, 16, 384), BF16),
            pltpu.VMEM((3, 128, 128), F32),
            pltpu.VMEM((8, 48, 512), BF16),
            pltpu.VMEM((8, 48, 640), BF16),
            pltpu.VMEM((8, 48, 128), BF16),
            pltpu.VMEM((8, 48, 128), BF16),
            pltpu.VMEM((8, 96, 384), BF16),
            pltpu.VMEM((8, 16, 384), BF16),
            pltpu.VMEM((8, 16, 512), BF16),
            pltpu.VMEM((4, 8, 16, 384), BF16),
            pltpu.VMEM((4, 8, 16, 512), BF16),
            pltpu.VMEM((7, 512, 128), F32),
            pltpu.VMEM((512, 128), F32),
            pltpu.VMEM((2, 2, 288, 512), BF16),
            pltpu.VMEM((2, 2, 288, 192), F32),
            pltpu.VMEM((2, 2, 288, 192), F32),
            pltpu.VMEM((2, 384, 768), BF16),
            pltpu.VMEM((2, 2, 512, 448), BF16),
            dma((9,)),
        ] + [dma((8,))] * 16 + [dma((4,))] * 4,
        compiler_params=pltpu.CompilerParams(
            collective_id=0, has_side_effects=True, vmem_limit_bytes=48 << 20),
        name="sink",
    )(*[pltpu.with_memory_space_constraint(a, pltpu.HBM) for a in (
        elemental.reshape(6, 192, 192), jnp.transpose(peramb_one, rows), jnp.transpose(peramb_two, rows),
        jnp.transpose(gen_peramb[0], rows),
    )])
    return out.reshape(1, 1, 2, 2, 3, 192, 192)


def solution(mesh):
    return jax.shard_map(
        body,
        mesh=mesh,
        in_specs=(
            P(None, None, "idx", None, None),
            P("spin", None, "idx", None),
            P("spin", None, "idx", None),
            P("cur", "spin", None, "idx", None),
        ),
        out_specs=P(None, "cur", "spin", None, "idx", None, None),
        check_vma=False,
    )
```

```python
import jax
import jax.numpy as jnp
from jax import lax
from jax.experimental import pallas as pl
from jax.experimental.pallas import tpu as pltpu
from jax.sharding import PartitionSpec as P

MESH = pl.DeviceIdType.MESH
F32, BF16 = jnp.float32, jnp.bfloat16
TN = (((0,), (0,)), ((), ()))
POWER = 32768.0
RELAY_V = True
RELAY_X = True
FAR_FIRST = (4, 3, 5, 2, 6, 1, 7)
SLOT = {1: 2, 2: 3, 3: 1}


def kernel(
    e_hbm, p_hbm, q_hbm, g_hbm, out_ref,
    e_ref, p_ref, q_ref, g_ref, e0, e1, ef, sel, qg0, qg1, qf,
    eba, ebb, psend, pbuf, qgbuf, xsa, xsb, xba, xbb, xf, xr, ah, zr, zi, qt, gw,
    in_sem, e1s, e1r, q1s, q1r, eas, ear, ebs, ebr, p2s, p2r, q2s, q2r,
    xas, xar, xbs, xbr, fas, far, fbs, fbr,
):
    idx, x, k = lax.axis_index("idx"), lax.axis_index("cur"), lax.axis_index("spin")
    y, z = idx // 8, idx % 8
    u = y * (1 - k) + z * k
    v = z * (1 - k) + y * k

    def column(uu, vv):
        return (uu * (1 - k) + vv * k) * 8 + vv * (1 - k) + uu * k

    def on_u(d):
        return (u + d) % 8

    def on_v(d):
        return (v + d) % 8

    started = []

    def send(src, dst, ss, rs, where):
        copy = pltpu.make_async_remote_copy(
            src_ref=src, dst_ref=dst, send_sem=ss, recv_sem=rs, device_id=where, device_id_type=MESH
        )
        copy.start()
        started.append(copy)
        return copy

    def to_u(d):
        return column(on_u(d), v), x, k

    def to_v(d):
        return column(u, on_v(d)), x, k

    loads = [
        pltpu.make_async_copy(src, dst, in_sem.at[i])
        for i, (src, dst) in enumerate(
            [(e_hbm.at[i], e_ref.at[i]) for i in range(6)] + [(p_hbm, p_ref), (q_hbm, q_ref), (g_hbm, g_ref)])
    ]
    for c in loads:
        c.start()
    barrier = pltpu.get_barrier_semaphore()
    for d in FAR_FIRST:
        pl.semaphore_signal(barrier, inc=1, device_id=to_u(d), device_id_type=MESH)
        pl.semaphore_signal(barrier, inc=1, device_id=to_v(d), device_id_type=MESH)
    for d in (2, 1, 3):
        pl.semaphore_signal(barrier, inc=1, device_id=(idx, (x + d) % 4, k), device_id_type=MESH)

    row = lax.broadcasted_iota(jnp.int32, (64, 1), 0)
    uu, beta = row >> 3, row & 7
    h = jnp.where(beta >= 3, 1, 0)
    t = beta - 3 * h
    source = 24 * (uu * (1 - k) + (2 * x + h) * k) + 3 * ((2 * x + h) * (1 - k) + uu * k) + t
    source = jnp.where(beta < 6, source, -1)
    pick_e = jnp.where(source == lax.broadcasted_iota(jnp.int32, (64, 192), 1), 1.0, 0.0).astype(BF16)
    loads[6].wait()
    p = p_ref[...].astype(F32)
    place = lax.broadcasted_iota(jnp.int32, (64, 192), 0) & 7
    picked = []
    for i in range(6):
        loads[i].wait()
        rows = jnp.dot(pick_e, e_ref[i], preferred_element_type=F32)
        for s in range(2):
            rows = jnp.where(place == 6 + s, p[s, i // 2, i % 2:i % 2 + 1, :], rows)
        picked.append(rows)
    e0[...] = jnp.concatenate(
        [m[:, :128].reshape(8, 8, 128) for m in picked]
        + [
            jnp.concatenate([picked[2 * i][:, 128:], picked[2 * i + 1][:, 128:]], axis=1).reshape(8, 8, 128)
            for i in range(3)
        ]
        + [jnp.zeros((8, 8, 128), F32)], axis=1).astype(BF16)
    pl.semaphore_wait(barrier, 17)

    e_sends = [send(e0.at[on_u(d)], e1.at[u], e1s.at[d - 1], e1r.at[d - 1], to_u(d)) for d in FAR_FIRST]
    for c in loads[7:]:
        c.wait()
    qg0[...] = jnp.concatenate([
        jnp.concatenate([a[s, :, r, :] for s in range(2) for r in range(2)] + [jnp.zeros((4, 192), F32)], axis=0)
        for a in (q_ref[...].astype(F32), g_ref[...].astype(F32))
    ], axis=1).astype(BF16)
    e1[u] = e0[u]
    qg1[u] = qg0[...]
    q_sends = [send(qg0, qg1.at[u], q1s.at[d - 1], q1r.at[d - 1], to_u(d)) for d in FAR_FIRST]
    n = lax.broadcasted_iota(jnp.int32, (1, 1024), 1)
    nv, nu, nt = n >> 7, (n >> 4) & 7, (n >> 2) & 3
    owner = 8 * (nu * (1 - k) + nv * k) + nv * (1 - k) + nu * k
    wanted = jnp.where(nt < 3, 3 * owner + nt + 192 * (n & 3), -1)
    at = lax.broadcasted_iota(jnp.int32, (128, 1), 0)
    for i in range(6):
        if i < 4:
            key = 192 * i + at
        else:
            key = 192 * (2 * (i - 4) + (at >> 6)) + 128 + (at & 63)
        sel[128 * i:128 * i + 128, :] = jnp.where(key == wanted, 1.0, 0.0).astype(BF16)

    left = lax.broadcasted_iota(jnp.int32, (8, 128), 1) < 64

    def tile(m):
        j, m = m // 3, m % 3
        pieces = []
        for i in range(6):
            if m < 2:
                pieces.append(ef[pl.ds(8 * i + 2 * j + m, 8, stride=80), :])
                continue
            first, second = [ef[pl.ds(48 + 8 * (i // 2) + 2 * j + b, 8, stride=80), :] for b in range(2)]
            if i % 2 == 0:
                second = pltpu.roll(second, 64, 1)
            else:
                first = pltpu.roll(first, 64, 1)
            pieces.append(jnp.where(left, first, second))
        return jnp.concatenate(pieces, axis=0).astype(BF16)

    for c in e_sends:
        c.wait_recv()
    ef[...] = e1[...].astype(F32).reshape(640, 128)
    for m in range(4):
        eba[v, :, pl.ds(128 * m, 128)] = tile(m)
    def first_leg(block, ss, rs):
        return {
            d: send(block.at[v], block.at[v], ss.at[d - 1], rs.at[d - 1], to_v(d))
            for d in ((2, 6, 1, 7) if RELAY_V else FAR_FIRST)
        }

    def second_leg(block, cut, sent, ss, rs):
        if not RELAY_V:
            return []
        size = block.shape[2]
        more = []
        for d, near, lanes, place in ((2, 1, pl.ds(0, cut), 3), (6, 7, pl.ds(cut, size - cut), 7)):
            sent[d].wait_recv()
            came = (v - d + 8) % 8
            whole, part = block.at[came], block.at[came, :, lanes]
            more.append(send(whole, whole, ss.at[2 if d == 2 else 4], rs.at[2 if d == 2 else 4], to_v(near)))
            more.append(send(part, part, ss.at[place], rs.at[place], to_v(d)))
        return [sent[1], sent[7]] + more

    a_sent = first_leg(eba, eas, ear)
    lhs = []
    for r in range(2):
        for i in range(3):
            tiles = []
            for s in range(2):
                pr, pi = [ef[pl.ds(8 * (2 * i + c) + 6 + s, 8, stride=80), :] for c in range(2)]
                tiles += [pr, pi] if r == 0 else [-pi, pr]
            for s in range(2):
                both = ef[pl.ds(48 + 8 * i + 6 + s, 8, stride=80), :]
                if r == 1:
                    both = pltpu.roll(both, 64, 1)
                    both = jnp.where(left, -both, both)
                tiles.append(both)
            lhs.append(jnp.concatenate(tiles, axis=1))
    chosen = jnp.dot(jnp.concatenate(lhs, axis=0).astype(BF16), sel[...], preferred_element_type=F32).astype(BF16)
    for i in range(8):
        psend[i] = chosen[:, 128 * i:128 * i + 128]
    a_sends = [send(psend.at[on_v(d)], pbuf.at[v], p2s.at[d - 1], p2r.at[d - 1], to_v(d)) for d in FAR_FIRST]
    pbuf[v] = psend[v]
    for m in range(5):
        ebb[v, :, pl.ds(128 * m, 128)] = tile(4 + m)
    b_sent = first_leg(ebb, ebs, ebr)
    if RELAY_V:
        a_sends += second_leg(eba, 256, a_sent, eas, ear)
        b_sends = second_leg(ebb, 384, b_sent, ebs, ebr)
    else:
        a_sends += list(a_sent.values())
        b_sends = list(b_sent.values())

    weights = None

    def contract(part, tiles):
        value = lax.dot_general(weights, part[...].reshape(384, 128 * tiles), TN, preferred_element_type=F32)
        largest = jnp.maximum(jnp.max(jnp.abs(value)), 1e-30)
        largest = jnp.full((8, 8, 128), largest, F32).astype(BF16).astype(F32)
        halves = []
        for m in range(tiles):
            scaled = value[:, 128 * m:128 * m + 128].reshape(8, 2, 8, 128)
            pair = []
            for i in range(2):
                a = scaled[:, i] * (POWER / largest)
                square = a * a
                fourth = square * square
                pair.append(jnp.where(a < 0, -fourth, fourth) * fourth)
            halves.append(pair)
        return halves, largest

    def along_x(block, there, here, part, sem, ss, rs, s):
        return send(block.at[here, part], block.at[there, part], ss.at[sem], rs.at[sem], (idx, (x + s) % 4, k))

    def spread_x(block, ss, rs, planes=(1, 3)):
        return {
            s: along_x(block, SLOT[s], 0, pl.ds(0, 8), s - 1, ss, rs, s) for s in planes
        }

    def pass_x(block, sent, ss, rs):
        for s in (1, 3):
            sent[s].wait_recv()
        if 2 in sent:
            return [sent[2]]
        if not RELAY_X:
            return [sent[2]]
        return [
            along_x(block, 3, 2, pl.ds(0, 4), 1, ss, rs, 1), along_x(block, 3, 1, pl.ds(4, 4), 3, ss, rs, 3)
        ]

    def decode(i):
        for m in range(7):
            code = (xba[i, :, :, 128 * m:128 * m + 128] if m < 3 else xbb[i, :, :, 128 * m - 384:128 * m - 256])
            code = code.astype(F32).reshape(128, 128)
            if m == 6:
                xr[pl.ds(128 * i, 128)] = code
            root = lax.rsqrt(jnp.maximum(jnp.abs(code), 1.2e-38))
            fourth = lax.rsqrt(root)
            size = fourth * lax.rsqrt(fourth)
            xf[m, pl.ds(128 * i, 128)] = jnp.where(code < 0, -size, size)

    low_rows = lax.broadcasted_iota(jnp.int32, (8, 8, 128), 1) < 4

    def third(pair, t):
        return pair[0] if t == 1 else pltpu.roll(pair[t // 2], 4, 1)

    def put(dst, m, first, second):
        dst[:, :, 128 * m:128 * m + 128] = jnp.concatenate([first, second], axis=1).astype(BF16)

    for c in a_sends:
        c.wait_recv()
    weights = pbuf[...].reshape(384, 128)
    halves, scale_a = contract(eba, 4)
    for m in range(3):
        put(xsa, m, halves[m][0], jnp.where(low_rows, halves[m][1], third(halves[3], m)))
    xa_sends = [
        send(xsa.at[on_u(d)], xba.at[0, u], xas.at[d - 1], xar.at[d - 1], to_u(d)) for d in FAR_FIRST
    ]
    xba[0, u] = xsa[u]
    for c in b_sends:
        c.wait_recv()
    halves, scale_b = contract(ebb, 5)
    for m in range(3):
        put(xsb, m, halves[m][0], jnp.where(low_rows, halves[m][1], third(halves[4], m)))
    sub = lax.broadcasted_iota(jnp.int32, (8, 8, 128), 1)
    put(xsb, 3, halves[3][0], jnp.where(low_rows, halves[3][1], jnp.where(sub == 4, scale_a, scale_b)))
    xb_sends = [
        send(xsb.at[on_u(d)], xbb.at[0, u], xbs.at[d - 1], xbr.at[d - 1], to_u(d)) for d in FAR_FIRST
    ]
    xbb[0, u] = xsb[u]

    for c in q_sends:
        c.wait_recv()
    for i in range(3):
        qf[i] = qg1[:, :, 128 * i:128 * i + 128].astype(F32).reshape(128, 128)
        qgbuf[v, :, pl.ds(128 * i, 128)] = jnp.concatenate(
            [qf[i, pl.ds(r, 8, stride=16), :] for r in range(12)], axis=0).astype(BF16)
    qg_sent = first_leg(qgbuf, q2s, q2r)
    for c in xa_sends:
        c.wait_recv()
    fa_sends = spread_x(xba, fas, far)
    qg_sends = second_leg(qgbuf, 256, qg_sent, q2s, q2r)
    for c in xb_sends:
        c.wait_recv()
    fb_sends = spread_x(xbb, fbs, fbr, (1, 3, 2))
    fa_more = pass_x(xba, fa_sends, fas, far)
    fb_more = pass_x(xbb, fb_sends, fbs, fbr)
    for i in (0, 1, 2):
        decode(i)
    received = lax.broadcasted_iota(jnp.int32, (192, 1), 0)
    wanted = lax.broadcasted_iota(jnp.int32, (192, 192), 1)
    rv, rt, ru = received // 24, received // 8 % 3, received % 8
    natural = rt + 3 * (rv * (1 - k) + ru * k) + 24 * (ru * (1 - k) + rv * k)
    place_g = jnp.where(natural == wanted, 1.0, 0.0).astype(BF16)
    beta = 3 * (rv % 2) + rt
    ahead = (rv // 2 - x + 4) % 4
    slot = jnp.where(ahead < 2, ahead, 5 - ahead)
    order = (beta % 2) * 96 + (slot // 2) * 48 + (beta // 2) * 16 + (slot % 2) * 8 + ru
    place_q = jnp.where(order == wanted, 1.0, 0.0).astype(BF16)
    none = jnp.zeros((64, 192), BF16)
    gw[:, :, :, 128:256] = jnp.zeros((2, 2, 512, 128), BF16)
    for c in qg_sends:
        c.wait_recv()

    for s in range(2):
        qs, gs = [], []
        for r in range(2):
            part = jnp.concatenate(
                [qgbuf[i, pl.ds(48 * s + 24 * r, 24), :].astype(F32) for i in range(8)], axis=0).astype(BF16)
            qs.append(lax.dot_general(part[:, :192], place_q, TN, preferred_element_type=F32).astype(BF16))
            gs.append(lax.dot_general(place_g, part[:, 192:], TN, preferred_element_type=F32).astype(BF16))
        qr, qi = qs
        for i in (0, 384):
            qt[s, :192, i:i + 192], qt[s, :192, i + 192:i + 384] = qr, -qi
            qt[s, 192:, i:i + 192], qt[s, 192:, i + 192:i + 384] = qi, qr
        for odd in range(2):
            gr, gi = [
                jnp.concatenate([m[:128], none, m[128:]] if odd else [m, none], axis=0) for m in gs
            ]
            gw[s, odd, :256, :192], gw[s, odd, 256:, :192] = gr, -gi
            gw[s, odd, :256, 256:], gw[s, odd, 256:, 256:] = gi, gr

    for half in range(2):
        if half == 1:
            for c in fa_more + fb_more:
                c.wait_recv()
            decode(3)
        scales = [xr[pl.ds(256 * half + 12 + i, 16, stride=16), :] * (1.0 / POWER) for i in range(2)]
        for s in range(2):
            for t in range(3):
                for r in range(2):
                    for m in range(9):
                        if m in (3, 8):
                            place, row = t if m == 3 else 3 + t, 12 + 2 * s + r
                        else:
                            place, row = m if m < 3 else m - 1, 4 * t + 2 * s + r
                        j, kind = m // 3, m % 3
                        code = xf[place, pl.ds(256 * half + row, 16, stride=16), :]
                        value = code * scales[0 if m < 4 else 1]
                        high = value.astype(BF16)
                        low = (value - high.astype(F32)).astype(BF16)
                        at = pl.ds(48 * t + 16 * j, 16)
                        for odd in range(2):
                            if kind in (odd, 2):
                                lane = pl.ds(256 * r + (128 if kind == 2 else 0), 128)
                                ah[s, odd, at, lane] = high
                                ah[s, odd, pl.ds(144 + 48 * t + 16 * j, 16), lane] = low
        for s in range(2):
            for odd in range(2):
                both = jnp.dot(ah[s, odd], gw[s, odd], preferred_element_type=F32)
                both = both[:144] + both[144:]
                zr[s, odd, pl.ds(144 * half, 144)] = both[:, :192]
                zi[s, odd, pl.ds(144 * half, 144)] = both[:, 256:]

    for s in range(2):
        for t in range(3):
            zc = jnp.concatenate([
                m[s, odd, pl.ds(144 * half + 48 * t, 48)] for m in (zr, zi) for odd in range(2) for half in range(2)
            ], axis=0)
            high = zc.astype(BF16)
            low = (zc - high.astype(F32)).astype(BF16)
            done = jnp.dot(qt[s], jnp.concatenate([high, low], axis=0), preferred_element_type=F32)
            for r in range(2):
                out_ref[s, r, t] = done[192 * r:192 * r + 192]
    for c in started:
        c.wait_send()


def body(elemental, peramb_one, peramb_two, gen_peramb):
    dma = pltpu.SemaphoreType.DMA
    vmem = pl.BlockSpec(memory_space=pltpu.VMEM)
    rows = (0, 2, 1, 3)
    out = pl.pallas_call(
        kernel,
        out_shape=jax.ShapeDtypeStruct((2, 2, 3, 192, 192), F32),
        in_specs=[pl.BlockSpec(memory_space=pltpu.HBM)] * 4,
        out_specs=vmem,
        scratch_shapes=[
            pltpu.VMEM((6, 192, 192), BF16),
            pltpu.VMEM((2, 3, 2, 192), BF16),
            pltpu.VMEM((2, 3, 2, 192), BF16),
            pltpu.VMEM((2, 3, 2, 192), BF16),
            pltpu.VMEM((8, 80, 128), BF16),
            pltpu.VMEM((8, 80, 128), BF16),
            pltpu.VMEM((640, 128), F32),
            pltpu.VMEM((768, 1024), BF16),
            pltpu.VMEM((16, 384), BF16),
            pltpu.VMEM((8, 16, 384), BF16),
            pltpu.VMEM((3, 128, 128), F32),
            pltpu.VMEM((8, 48, 512), BF16),
            pltpu.VMEM((8, 48, 640), BF16),
            pltpu.VMEM((8, 48, 128), BF16),
            pltpu.VMEM((8, 48, 128), BF16),
            pltpu.VMEM((8, 96, 384), BF16),
            pltpu.VMEM((8, 16, 384), BF16),
            pltpu.VMEM((8, 16, 512), BF16),
            pltpu.VMEM((4, 8, 16, 384), BF16),
            pltpu.VMEM((4, 8, 16, 512), BF16),
            pltpu.VMEM((7, 512, 128), F32),
            pltpu.VMEM((512, 128), F32),
            pltpu.VMEM((2, 2, 288, 512), BF16),
            pltpu.VMEM((2, 2, 288, 192), F32),
            pltpu.VMEM((2, 2, 288, 192), F32),
            pltpu.VMEM((2, 384, 768), BF16),
            pltpu.VMEM((2, 2, 512, 448), BF16),
            dma((9,)),
        ] + [dma((8,))] * 16 + [dma((4,))] * 4,
        compiler_params=pltpu.CompilerParams(
            collective_id=0, has_side_effects=True, vmem_limit_bytes=48 << 20),
        name="sink",
    )(*[pltpu.with_memory_space_constraint(a, pltpu.HBM) for a in (
        elemental.reshape(6, 192, 192), jnp.transpose(peramb_one, rows), jnp.transpose(peramb_two, rows),
        jnp.transpose(gen_peramb[0], rows),
    )])
    return out.reshape(1, 1, 2, 2, 3, 192, 192)


def solution(mesh):
    return jax.shard_map(
        body,
        mesh=mesh,
        in_specs=(
            P(None, None, "idx", None, None),
            P("spin", None, "idx", None),
            P("spin", None, "idx", None),
            P("cur", "spin", None, "idx", None),
        ),
        out_specs=P(None, "cur", "spin", None, "idx", None, None),
        check_vma=False,
    )
```

```python
import jax
import jax.numpy as jnp
from jax import lax
from jax.experimental import pallas as pl
from jax.experimental.pallas import tpu as pltpu
from jax.sharding import PartitionSpec as P

MESH = pl.DeviceIdType.MESH
F32, BF16 = jnp.float32, jnp.bfloat16
TN = (((0,), (0,)), ((), ()))
POWER = 32768.0
RELAY_V = True
RELAY_X = True
FAR_FIRST = (4, 3, 5, 2, 6, 1, 7)
SLOT = {1: 2, 2: 3, 3: 1}


def kernel(
    e_hbm, p_hbm, q_hbm, g_hbm, out_ref,
    e_ref, p_ref, q_ref, g_ref, e0, e1, ef, sel, qg0, qg1, qf,
    eba, ebb, psend, pbuf, qgbuf, xsa, xsb, xba, xbb, xf, xr, ah, zr, zi, qt, gw,
    in_sem, e1s, e1r, q1s, q1r, eas, ear, ebs, ebr, p2s, p2r, q2s, q2r,
    xas, xar, xbs, xbr, fas, far, fbs, fbr,
):
    idx, x, k = lax.axis_index("idx"), lax.axis_index("cur"), lax.axis_index("spin")
    y, z = idx // 8, idx % 8
    u = y * (1 - k) + z * k
    v = z * (1 - k) + y * k

    def column(uu, vv):
        return (uu * (1 - k) + vv * k) * 8 + vv * (1 - k) + uu * k

    def on_u(d):
        return (u + d) % 8

    def on_v(d):
        return (v + d) % 8

    started = []

    def send(src, dst, ss, rs, where):
        copy = pltpu.make_async_remote_copy(
            src_ref=src, dst_ref=dst, send_sem=ss, recv_sem=rs, device_id=where, device_id_type=MESH
        )
        copy.start()
        started.append(copy)
        return copy

    def to_u(d):
        return column(on_u(d), v), x, k

    def to_v(d):
        return column(u, on_v(d)), x, k

    loads = [
        pltpu.make_async_copy(src, dst, in_sem.at[i])
        for i, (src, dst) in enumerate(
            [(e_hbm.at[i], e_ref.at[i]) for i in range(6)] + [(p_hbm, p_ref), (q_hbm, q_ref), (g_hbm, g_ref)])
    ]
    for c in loads:
        c.start()
    barrier = pltpu.get_barrier_semaphore()
    for d in FAR_FIRST:
        pl.semaphore_signal(barrier, inc=1, device_id=to_u(d), device_id_type=MESH)
        pl.semaphore_signal(barrier, inc=1, device_id=to_v(d), device_id_type=MESH)
    for d in (2, 1, 3):
        pl.semaphore_signal(barrier, inc=1, device_id=(idx, (x + d) % 4, k), device_id_type=MESH)

    row = lax.broadcasted_iota(jnp.int32, (64, 1), 0)
    uu, beta = row >> 3, row & 7
    h = jnp.where(beta >= 3, 1, 0)
    t = beta - 3 * h
    source = 24 * (uu * (1 - k) + (2 * x + h) * k) + 3 * ((2 * x + h) * (1 - k) + uu * k) + t
    source = jnp.where(beta < 6, source, -1)
    pick_e = jnp.where(source == lax.broadcasted_iota(jnp.int32, (64, 192), 1), 1.0, 0.0).astype(BF16)
    loads[6].wait()
    p = p_ref[...].astype(F32)
    place = lax.broadcasted_iota(jnp.int32, (64, 192), 0) & 7
    picked = []
    for i in range(6):
        loads[i].wait()
        rows = jnp.dot(pick_e, e_ref[i], preferred_element_type=F32)
        for s in range(2):
            rows = jnp.where(place == 6 + s, p[s, i // 2, i % 2:i % 2 + 1, :], rows)
        picked.append(rows)
    e0[...] = jnp.concatenate(
        [m[:, :128].reshape(8, 8, 128) for m in picked]
        + [
            jnp.concatenate([picked[2 * i][:, 128:], picked[2 * i + 1][:, 128:]], axis=1).reshape(8, 8, 128)
            for i in range(3)
        ]
        + [jnp.zeros((8, 8, 128), F32)], axis=1).astype(BF16)
    pl.semaphore_wait(barrier, 17)

    e_sends = [send(e0.at[on_u(d)], e1.at[u], e1s.at[d - 1], e1r.at[d - 1], to_u(d)) for d in FAR_FIRST]
    for c in loads[7:]:
        c.wait()
    qg0[...] = jnp.concatenate([
        jnp.concatenate([a[s, :, r, :] for s in range(2) for r in range(2)] + [jnp.zeros((4, 192), F32)], axis=0)
        for a in (q_ref[...].astype(F32), g_ref[...].astype(F32))
    ], axis=1).astype(BF16)
    e1[u] = e0[u]
    qg1[u] = qg0[...]
    q_sends = [send(qg0, qg1.at[u], q1s.at[d - 1], q1r.at[d - 1], to_u(d)) for d in FAR_FIRST]
    n = lax.broadcasted_iota(jnp.int32, (1, 1024), 1)
    nv, nu, nt = n >> 7, (n >> 4) & 7, (n >> 2) & 3
    owner = 8 * (nu * (1 - k) + nv * k) + nv * (1 - k) + nu * k
    wanted = jnp.where(nt < 3, 3 * owner + nt + 192 * (n & 3), -1)
    at = lax.broadcasted_iota(jnp.int32, (128, 1), 0)
    for i in range(6):
        if i < 4:
            key = 192 * i + at
        else:
            key = 192 * (2 * (i - 4) + (at >> 6)) + 128 + (at & 63)
        sel[128 * i:128 * i + 128, :] = jnp.where(key == wanted, 1.0, 0.0).astype(BF16)

    left = lax.broadcasted_iota(jnp.int32, (8, 128), 1) < 64

    def tile(m):
        j, m = m // 3, m % 3
        pieces = []
        for i in range(6):
            if m < 2:
                pieces.append(ef[pl.ds(8 * i + 2 * j + m, 8, stride=80), :])
                continue
            first, second = [ef[pl.ds(48 + 8 * (i // 2) + 2 * j + b, 8, stride=80), :] for b in range(2)]
            if i % 2 == 0:
                second = pltpu.roll(second, 64, 1)
            else:
                first = pltpu.roll(first, 64, 1)
            pieces.append(jnp.where(left, first, second))
        return jnp.concatenate(pieces, axis=0).astype(BF16)

    for c in e_sends:
        c.wait_recv()
    ef[...] = e1[...].astype(F32).reshape(640, 128)
    for m in range(4):
        eba[v, :, pl.ds(128 * m, 128)] = tile(m)
    def first_leg(block, ss, rs):
        return {
            d: send(block.at[v], block.at[v], ss.at[d - 1], rs.at[d - 1], to_v(d))
            for d in ((2, 6, 1, 7) if RELAY_V else FAR_FIRST)
        }

    def second_leg(block, cut, sent, ss, rs):
        if not RELAY_V:
            return []
        size = block.shape[2]
        more = []
        for d, near, lanes, place in ((2, 1, pl.ds(0, cut), 3), (6, 7, pl.ds(cut, size - cut), 7)):
            sent[d].wait_recv()
            came = (v - d + 8) % 8
            whole, part = block.at[came], block.at[came, :, lanes]
            more.append(send(part, part, ss.at[place], rs.at[place], to_v(d)))
            more.append(send(whole, whole, ss.at[2 if d == 2 else 4], rs.at[2 if d == 2 else 4], to_v(near)))
        return [sent[1], sent[7]] + more

    a_sent = first_leg(eba, eas, ear)
    lhs = []
    for r in range(2):
        for i in range(3):
            tiles = []
            for s in range(2):
                pr, pi = [ef[pl.ds(8 * (2 * i + c) + 6 + s, 8, stride=80), :] for c in range(2)]
                tiles += [pr, pi] if r == 0 else [-pi, pr]
            for s in range(2):
                both = ef[pl.ds(48 + 8 * i + 6 + s, 8, stride=80), :]
                if r == 1:
                    both = pltpu.roll(both, 64, 1)
                    both = jnp.where(left, -both, both)
                tiles.append(both)
            lhs.append(jnp.concatenate(tiles, axis=1))
    chosen = jnp.dot(jnp.concatenate(lhs, axis=0).astype(BF16), sel[...], preferred_element_type=F32).astype(BF16)
    for i in range(8):
        psend[i] = chosen[:, 128 * i:128 * i + 128]
    a_sends = [send(psend.at[on_v(d)], pbuf.at[v], p2s.at[d - 1], p2r.at[d - 1], to_v(d)) for d in FAR_FIRST]
    pbuf[v] = psend[v]
    for m in range(5):
        ebb[v, :, pl.ds(128 * m, 128)] = tile(4 + m)
    b_sent = first_leg(ebb, ebs, ebr)
    if RELAY_V:
        a_sends += second_leg(eba, 256, a_sent, eas, ear)
        b_sends = second_leg(ebb, 384, b_sent, ebs, ebr)
    else:
        a_sends += list(a_sent.values())
        b_sends = list(b_sent.values())

    weights = None

    def contract(part, tiles):
        value = lax.dot_general(weights, part[...].reshape(384, 128 * tiles), TN, preferred_element_type=F32)
        largest = jnp.maximum(jnp.max(jnp.abs(value)), 1e-30)
        largest = jnp.full((8, 8, 128), largest, F32).astype(BF16).astype(F32)
        halves = []
        for m in range(tiles):
            scaled = value[:, 128 * m:128 * m + 128].reshape(8, 2, 8, 128)
            pair = []
            for i in range(2):
                a = scaled[:, i] * (POWER / largest)
                square = a * a
                fourth = square * square
                pair.append(jnp.where(a < 0, -fourth, fourth) * fourth)
            halves.append(pair)
        return halves, largest

    def along_x(block, there, here, part, sem, ss, rs, s):
        return send(block.at[here, part], block.at[there, part], ss.at[sem], rs.at[sem], (idx, (x + s) % 4, k))

    def spread_x(block, ss, rs):
        return {
            s: along_x(block, SLOT[s], 0, pl.ds(0, 8), s - 1, ss, rs, s) for s in ((1, 3) if RELAY_X else (2, 1, 3))
        }

    def pass_x(block, sent, ss, rs):
        for s in (1, 3):
            sent[s].wait_recv()
        if not RELAY_X:
            return [sent[2]]
        return [
            along_x(block, 3, 2, pl.ds(0, 4), 1, ss, rs, 1), along_x(block, 3, 1, pl.ds(4, 4), 3, ss, rs, 3)
        ]

    def decode(i):
        for m in range(7):
            code = (xba[i, :, :, 128 * m:128 * m + 128] if m < 3 else xbb[i, :, :, 128 * m - 384:128 * m - 256])
            code = code.astype(F32).reshape(128, 128)
            if m == 6:
                xr[pl.ds(128 * i, 128)] = code
            root = lax.rsqrt(jnp.maximum(jnp.abs(code), 1.2e-38))
            fourth = lax.rsqrt(root)
            size = fourth * lax.rsqrt(fourth)
            xf[m, pl.ds(128 * i, 128)] = jnp.where(code < 0, -size, size)

    low_rows = lax.broadcasted_iota(jnp.int32, (8, 8, 128), 1) < 4

    def third(pair, t):
        return pair[0] if t == 1 else pltpu.roll(pair[t // 2], 4, 1)

    def put(dst, m, first, second):
        dst[:, :, 128 * m:128 * m + 128] = jnp.concatenate([first, second], axis=1).astype(BF16)

    for c in a_sends:
        c.wait_recv()
    weights = pbuf[...].reshape(384, 128)
    halves, scale_a = contract(eba, 4)
    for m in range(3):
        put(xsa, m, halves[m][0], jnp.where(low_rows, halves[m][1], third(halves[3], m)))
    xa_sends = [
        send(xsa.at[on_u(d)], xba.at[0, u], xas.at[d - 1], xar.at[d - 1], to_u(d)) for d in FAR_FIRST
    ]
    xba[0, u] = xsa[u]
    for c in b_sends:
        c.wait_recv()
    halves, scale_b = contract(ebb, 5)
    for m in range(3):
        put(xsb, m, halves[m][0], jnp.where(low_rows, halves[m][1], third(halves[4], m)))
    sub = lax.broadcasted_iota(jnp.int32, (8, 8, 128), 1)
    put(xsb, 3, halves[3][0], jnp.where(low_rows, halves[3][1], jnp.where(sub == 4, scale_a, scale_b)))
    xb_sends = [
        send(xsb.at[on_u(d)], xbb.at[0, u], xbs.at[d - 1], xbr.at[d - 1], to_u(d)) for d in FAR_FIRST
    ]
    xbb[0, u] = xsb[u]

    for c in q_sends:
        c.wait_recv()
    for i in range(3):
        qf[i] = qg1[:, :, 128 * i:128 * i + 128].astype(F32).reshape(128, 128)
        qgbuf[v, :, pl.ds(128 * i, 128)] = jnp.concatenate(
            [qf[i, pl.ds(r, 8, stride=16), :] for r in range(12)], axis=0).astype(BF16)
    qg_sent = first_leg(qgbuf, q2s, q2r)
    for c in xa_sends:
        c.wait_recv()
    fa_sends = spread_x(xba, fas, far)
    qg_sends = second_leg(qgbuf, 256, qg_sent, q2s, q2r)
    for c in xb_sends:
        c.wait_recv()
    fb_sends = spread_x(xbb, fbs, fbr)
    fa_more = pass_x(xba, fa_sends, fas, far)
    fb_more = pass_x(xbb, fb_sends, fbs, fbr)
    for i in (0, 1, 2):
        decode(i)
    received = lax.broadcasted_iota(jnp.int32, (192, 1), 0)
    wanted = lax.broadcasted_iota(jnp.int32, (192, 192), 1)
    rv, rt, ru = received // 24, received // 8 % 3, received % 8
    natural = rt + 3 * (rv * (1 - k) + ru * k) + 24 * (ru * (1 - k) + rv * k)
    place_g = jnp.where(natural == wanted, 1.0, 0.0).astype(BF16)
    beta = 3 * (rv % 2) + rt
    ahead = (rv // 2 - x + 4) % 4
    slot = jnp.where(ahead < 2, ahead, 5 - ahead)
    order = (beta % 2) * 96 + (slot // 2) * 48 + (beta // 2) * 16 + (slot % 2) * 8 + ru
    place_q = jnp.where(order == wanted, 1.0, 0.0).astype(BF16)
    none = jnp.zeros((64, 192), BF16)
    gw[:, :, :, 128:256] = jnp.zeros((2, 2, 512, 128), BF16)
    for c in qg_sends:
        c.wait_recv()

    for s in range(2):
        qs, gs = [], []
        for r in range(2):
            part = jnp.concatenate(
                [qgbuf[i, pl.ds(48 * s + 24 * r, 24), :].astype(F32) for i in range(8)], axis=0).astype(BF16)
            qs.append(lax.dot_general(part[:, :192], place_q, TN, preferred_element_type=F32).astype(BF16))
            gs.append(lax.dot_general(place_g, part[:, 192:], TN, preferred_element_type=F32).astype(BF16))
        qr, qi = qs
        for i in (0, 384):
            qt[s, :192, i:i + 192], qt[s, :192, i + 192:i + 384] = qr, -qi
            qt[s, 192:, i:i + 192], qt[s, 192:, i + 192:i + 384] = qi, qr
        for odd in range(2):
            gr, gi = [
                jnp.concatenate([m[:128], none, m[128:]] if odd else [m, none], axis=0) for m in gs
            ]
            gw[s, odd, :256, :192], gw[s, odd, 256:, :192] = gr, -gi
            gw[s, odd, :256, 256:], gw[s, odd, 256:, 256:] = gi, gr

    for half in range(2):
        if half == 1:
            for c in fa_more + fb_more:
                c.wait_recv()
            decode(3)
        scales = [xr[pl.ds(256 * half + 12 + i, 16, stride=16), :] * (1.0 / POWER) for i in range(2)]
        for s in range(2):
            for t in range(3):
                for r in range(2):
                    for m in range(9):
                        if m in (3, 8):
                            place, row = t if m == 3 else 3 + t, 12 + 2 * s + r
                        else:
                            place, row = m if m < 3 else m - 1, 4 * t + 2 * s + r
                        j, kind = m // 3, m % 3
                        code = xf[place, pl.ds(256 * half + row, 16, stride=16), :]
                        value = code * scales[0 if m < 4 else 1]
                        high = value.astype(BF16)
                        low = (value - high.astype(F32)).astype(BF16)
                        at = pl.ds(48 * t + 16 * j, 16)
                        for odd in range(2):
                            if kind in (odd, 2):
                                lane = pl.ds(256 * r + (128 if kind == 2 else 0), 128)
                                ah[s, odd, at, lane] = high
                                ah[s, odd, pl.ds(144 + 48 * t + 16 * j, 16), lane] = low
        for s in range(2):
            for odd in range(2):
                both = jnp.dot(ah[s, odd], gw[s, odd], preferred_element_type=F32)
                both = both[:144] + both[144:]
                zr[s, odd, pl.ds(144 * half, 144)] = both[:, :192]
                zi[s, odd, pl.ds(144 * half, 144)] = both[:, 256:]

    for s in range(2):
        for t in range(3):
            zc = jnp.concatenate([
                m[s, odd, pl.ds(144 * half + 48 * t, 48)] for m in (zr, zi) for odd in range(2) for half in range(2)
            ], axis=0)
            high = zc.astype(BF16)
            low = (zc - high.astype(F32)).astype(BF16)
            done = jnp.dot(qt[s], jnp.concatenate([high, low], axis=0), preferred_element_type=F32)
            for r in range(2):
                out_ref[s, r, t] = done[192 * r:192 * r + 192]
    for c in started:
        c.wait_send()


def body(elemental, peramb_one, peramb_two, gen_peramb):
    dma = pltpu.SemaphoreType.DMA
    vmem = pl.BlockSpec(memory_space=pltpu.VMEM)
    rows = (0, 2, 1, 3)
    out = pl.pallas_call(
        kernel,
        out_shape=jax.ShapeDtypeStruct((2, 2, 3, 192, 192), F32),
        in_specs=[pl.BlockSpec(memory_space=pltpu.HBM)] * 4,
        out_specs=vmem,
        scratch_shapes=[
            pltpu.VMEM((6, 192, 192), BF16),
            pltpu.VMEM((2, 3, 2, 192), BF16),
            pltpu.VMEM((2, 3, 2, 192), BF16),
            pltpu.VMEM((2, 3, 2, 192), BF16),
            pltpu.VMEM((8, 80, 128), BF16),
            pltpu.VMEM((8, 80, 128), BF16),
            pltpu.VMEM((640, 128), F32),
            pltpu.VMEM((768, 1024), BF16),
            pltpu.VMEM((16, 384), BF16),
            pltpu.VMEM((8, 16, 384), BF16),
            pltpu.VMEM((3, 128, 128), F32),
            pltpu.VMEM((8, 48, 512), BF16),
            pltpu.VMEM((8, 48, 640), BF16),
            pltpu.VMEM((8, 48, 128), BF16),
            pltpu.VMEM((8, 48, 128), BF16),
            pltpu.VMEM((8, 96, 384), BF16),
            pltpu.VMEM((8, 16, 384), BF16),
            pltpu.VMEM((8, 16, 512), BF16),
            pltpu.VMEM((4, 8, 16, 384), BF16),
            pltpu.VMEM((4, 8, 16, 512), BF16),
            pltpu.VMEM((7, 512, 128), F32),
            pltpu.VMEM((512, 128), F32),
            pltpu.VMEM((2, 2, 288, 512), BF16),
            pltpu.VMEM((2, 2, 288, 192), F32),
            pltpu.VMEM((2, 2, 288, 192), F32),
            pltpu.VMEM((2, 384, 768), BF16),
            pltpu.VMEM((2, 2, 512, 448), BF16),
            dma((9,)),
        ] + [dma((8,))] * 16 + [dma((4,))] * 4,
        compiler_params=pltpu.CompilerParams(
            collective_id=0, has_side_effects=True, vmem_limit_bytes=48 << 20),
        name="sink",
    )(*[pltpu.with_memory_space_constraint(a, pltpu.HBM) for a in (
        elemental.reshape(6, 192, 192), jnp.transpose(peramb_one, rows), jnp.transpose(peramb_two, rows),
        jnp.transpose(gen_peramb[0], rows),
    )])
    return out.reshape(1, 1, 2, 2, 3, 192, 192)


def solution(mesh):
    return jax.shard_map(
        body,
        mesh=mesh,
        in_specs=(
            P(None, None, "idx", None, None),
            P("spin", None, "idx", None),
            P("spin", None, "idx", None),
            P("cur", "spin", None, "idx", None),
        ),
        out_specs=P(None, "cur", "spin", None, "idx", None, None),
        check_vma=False,
    )
```
